32 devices in a mesh: pipe: 2 (over core), expert: 16 (over z, y, x).
Axes of the slice: x: 2, y: 2, z: 4, core: 2. Of those that a mesh axis runs over, the one named last changes fastest.
Arguments:
- act_a: bfloat16 [2, 1024, 3584], P('pipe', 'expert'), may hold values from -6 to 6
- ids_a: int32 [2, 1024, 2], P('pipe', 'expert'), may hold values from 0 to 3, all different within a row; in each aligned block of 64 rows (0 to 63, 64 to 127, ..., all dimensions but the last counted through in order) at most 40 rows name the same one
- act_b: bfloat16 [2, 1024, 3584], P('pipe', 'expert'), may hold values from -6 to 6
- cot_b: bfloat16 [2, 1024, 3584], P('pipe', 'expert'), may hold values from -6 to 6
- ids_b: int32 [2, 1024, 2], P('pipe', 'expert'), may hold values from 0 to 3, all different within a row; in each aligned block of 64 rows (0 to 63, 64 to 127, ..., all dimensions but the last counted through in order) at most 40 rows name the same one
- norm_gain: bfloat16 [2, 3584], P('pipe'), may hold values from 0.5 to 1.5
- router: bfloat16 [2, 3584, 4], P('pipe'), may hold values from -0.09375 to 0.09375
- w_gate: bfloat16 [2, 16, 3584, 256], P('pipe', 'expert'), may hold values from -0.09375 to 0.09375
- w_up: bfloat16 [2, 16, 3584, 256], P('pipe', 'expert'), may hold values from -0.09375 to 0.09375
- w_down: bfloat16 [2, 16, 256, 3584], P('pipe', 'expert'), may hold values from -0.1875 to 0.1875
Outputs:
- next_a: bfloat16 [2, 1024, 3584], P('pipe', 'expert')
- next_b: bfloat16 [2, 1024, 3584], P('pipe', 'expert')
The draws below stay inside these ranges and needn't reach their ends.
Inputs may be any that keep to these rules, and one draw needn't show every extreme that they name: `ids_a`: each row names 2 different experts. Within the 64 rows of one device (aligned blocks along the relay and token dimensions taken together) no expert is named by more than 40 rows, a bound that some block reaches of them. `ids_b`: as for ids_a.
All inputs are finite; a program needn't handle non-finite values.
Results may differ from the reference program's by a relative error of at most 0.013.
Values may be sent and summed in bfloat16 or wider, within the bound.
A program may use at most 128 MiB of HBM per device.

```python
import math
import jax
import jax.numpy as jnp
import numpy as np
from jax import lax

D = 3584
FF = 1024
SPLIT = 4
TOP = 2
TOK_DEV = 64
FF_DEV = 256
EXPERTS = 4
TOKENS = 1024
CAP = 40
N_PIPE = 2
N_EXPERT = 16


def shard_levels(rng, dims, split, smallest, largest):
    def one(position, blocks):
        draws = jax.random.uniform(jax.random.fold_in(jax.random.fold_in(rng, 6), position), (blocks,), jnp.float32, smallest / len(split), largest / len(split))
        return jnp.repeat(jnp.exp(draws), dims[position] // blocks).reshape((-1,) + (1,) * (len(dims) - position - 1))

    level = one(*split[0])
    for cut in split[1:]:
        level = level * one(*cut)
    return level


def deal_out(stream_key, own, number, rows, amount, top, bound, skew):
    order = jax.random.permutation(stream_key, amount)
    heavy_load, common = portions_of(amount, rows * top, bound, skew, True), portions_of(amount, rows * top, bound, skew, False)
    places = jnp.arange(amount)

    def named(sizes, rotation):
        used = int((sizes > 0).sum())
        fixed = max(1, used // 4)
        passed = fixed + (places - fixed + rotation * (used - fixed)) % max(1, amount - fixed)
        return jnp.zeros((amount,), jnp.int32).at[order[jnp.where(places < fixed, places, passed)]].set(jnp.asarray(sizes, jnp.int32))

    sizes = jnp.where(number % 4 == 0, named(heavy_load, number // 4), named(common, number - number // 4 - 1))
    mixed = jax.random.permutation(jax.random.fold_in(own, 3), amount)
    source_of, taker = mixed[0:amount // 2 * 2:2], mixed[1:amount // 2 * 2:2]
    room = jnp.minimum(sizes[source_of] - 1, bound - sizes[taker]) // 2
    room = jnp.where((source_of == order[0]) | (taker == order[0]) | (sizes[taker] == 0), 0, jnp.maximum(room, 0))
    passed = jax.random.randint(jax.random.fold_in(own, 4), (amount // 2,), 0, 1 << 20) % (room + 1)
    sizes = sizes.at[source_of].add(-passed).at[taker].add(passed)
    members = jnp.searchsorted(jnp.cumsum(sizes), jnp.arange(rows * top), side="right").astype(jnp.int32)
    grid = members.reshape(top, rows).T
    grid = grid[jax.random.permutation(jax.random.fold_in(own, 1), rows)]
    rotation = jax.random.randint(jax.random.fold_in(own, 2), (rows, 1), 0, top)
    return jnp.take_along_axis(grid, (jnp.arange(top)[None, :] + rotation) % top, axis=1)


def portions_of(number_of, total, bound, lean, full):
    loads = [(1 << 20) // math.isqrt(standing ** lean) + 1 for standing in range(1, number_of + 1)]
    largest = bound if full else min(bound, max(-(-total // number_of), total * loads[0] // sum(loads)))
    least = 1 if total - largest >= number_of - 1 else 0
    counts, rest = [largest] + [least] * (number_of - 1), total - largest - least * (number_of - 1)
    while rest > 0:
        free = [i for i in range(1, number_of) if counts[i] < largest] or [i for i in range(1, number_of) if counts[i] < bound]
        whole, remaining = sum([loads[i] for i in free]), rest
        for i in free:
            addition = min(bound - counts[i], max(1, remaining * loads[i] // whole), rest)
            counts[i] = counts[i] + addition
            rest = rest - addition
    return np.array(counts)


def gaussian(key, dims, deviation, limit, split=(), kind=jnp.bfloat16):
    result = jax.random.normal(key, dims, jnp.float32) * deviation
    if len(split) > 0:
        result = shard_levels(key, dims, split, -0.22, 0.18) * result
    return jnp.clip(result, min=-limit, max=limit).astype(kind)


def setup_inputs(seed: int = 0) -> dict:
    streams_of = jax.random.split(jax.random.key(seed), 11)
    act_a = gaussian(streams_of[0], (N_PIPE, TOKENS, D), 1.0, 6.0, ((0, 2), (1, 16)))
    ids_a_keys = jax.random.split(jax.random.fold_in(streams_of[1], 1), N_PIPE * TOKENS // TOK_DEV)
    ids_a_turns = jax.random.permutation(jax.random.fold_in(streams_of[1], 3), N_PIPE * TOKENS // TOK_DEV)
    ids_a = jax.vmap(lambda own, number: deal_out(jax.random.fold_in(streams_of[1], 2), own, number, TOK_DEV, EXPERTS, TOP, CAP, 2))(ids_a_keys, ids_a_turns).reshape((N_PIPE, TOKENS, TOP))
    act_b = gaussian(streams_of[2], (N_PIPE, TOKENS, D), 1.0, 6.0, ((0, 2), (1, 16)))
    cot_b = gaussian(streams_of[3], (N_PIPE, TOKENS, D), 1.0, 6.0, ((0, 2), (1, 16)))
    ids_b_keys = jax.random.split(jax.random.fold_in(streams_of[4], 1), N_PIPE * TOKENS // TOK_DEV)
    ids_b_turns = jax.random.permutation(jax.random.fold_in(streams_of[4], 3), N_PIPE * TOKENS // TOK_DEV)
    ids_b = jax.vmap(lambda own, number: deal_out(jax.random.fold_in(streams_of[4], 2), own, number, TOK_DEV, EXPERTS, TOP, CAP, 2))(ids_b_keys, ids_b_turns).reshape((N_PIPE, TOKENS, TOP))
    norm_gain = jnp.clip(1.0 + 0.1 * jax.random.normal(streams_of[5], (N_PIPE, D), jnp.float32), 0.5, 1.5).astype(jnp.bfloat16)
    router = gaussian(streams_of[6], (N_PIPE, D, EXPERTS), D ** -0.5, 0.09375, ((0, 2),))
    w_gate = gaussian(streams_of[7], (N_PIPE, N_EXPERT, D, FF_DEV), D ** -0.5, 0.09375, ((0, 2), (1, 16)))
    w_up = gaussian(streams_of[8], (N_PIPE, N_EXPERT, D, FF_DEV), D ** -0.5, 0.09375, ((0, 2), (1, 16)))
    w_down = gaussian(streams_of[9], (N_PIPE, N_EXPERT, FF_DEV, D), FF ** -0.5, 0.1875, ((0, 2), (1, 16)))
    return {"act_a": act_a, "ids_a": ids_a, "act_b": act_b, "cot_b": cot_b, "ids_b": ids_b, "norm_gain": norm_gain, "router": router, "w_gate": w_gate, "w_up": w_up, "w_down": w_down}


route_scale = 2.5
norm_eps = 1e-06

def normalize(inputs, gain_row):
    values = inputs.astype(jnp.float32)
    inverse = lax.rsqrt(lax.optimization_barrier(jnp.mean(values * values, axis=-1, keepdims=True)) + norm_eps)
    normed = (values * inverse * gain_row.astype(jnp.float32)).astype(jnp.bfloat16)
    return (normed, values, inverse)

def route_gates(normed, router_cols, expert_ids):
    logits = jnp.dot(normed, router_cols, preferred_element_type=jnp.float32)
    picker = expert_ids[:, :, None] == jnp.arange(router_cols.shape[1], dtype=jnp.int32)[None, None, :]
    chosen = lax.optimization_barrier(jnp.sum(jnp.where(picker, logits[:, None, :], 0.0), axis=2))
    scores = jax.nn.sigmoid(chosen)
    return (scores, scores / lax.optimization_barrier(jnp.sum(scores, axis=1, keepdims=True)), picker)

def expert_forward(rows_in, gate_w, up_w, down_w):
    gate_pre = jnp.dot(rows_in, gate_w, preferred_element_type=jnp.float32)
    up_pre = jnp.dot(rows_in, up_w, preferred_element_type=jnp.float32)
    sig_gate = jax.nn.sigmoid(gate_pre)
    activation = (gate_pre * sig_gate * up_pre).astype(jnp.bfloat16)
    output = jnp.dot(activation, down_w, preferred_element_type=jnp.float32).astype(jnp.bfloat16)
    return (output, gate_pre, up_pre, sig_gate)

def expert_backward(rows_in, grad_rows, gate_w, up_w, down_w):
    output, gate_pre, up_pre, sig_gate = expert_forward(rows_in, gate_w, up_w, down_w)
    contract = lax.optimization_barrier(jnp.sum(grad_rows.astype(jnp.float32) * output.astype(jnp.float32), axis=-1)).astype(jnp.bfloat16)
    last_dims = (((1,), (1,)), ((), ()))
    grad_act = lax.dot_general(grad_rows, down_w, last_dims, preferred_element_type=jnp.float32)
    grad_gate = (grad_act * up_pre * sig_gate * (1.0 + gate_pre * (1.0 - sig_gate))).astype(jnp.bfloat16)
    grad_up = (grad_act * gate_pre * sig_gate).astype(jnp.bfloat16)
    grad_in = lax.dot_general(grad_gate, gate_w, last_dims, preferred_element_type=jnp.float32)
    grad_in = grad_in + lax.dot_general(grad_up, up_w, last_dims, preferred_element_type=jnp.float32)
    return (grad_in.astype(jnp.bfloat16), contract)

def split_weights(gate_all, up_all, down_all):
    gate_set = gate_all.reshape(EXPERTS, SPLIT, gate_all.shape[1], gate_all.shape[2])
    up_set = up_all.reshape(EXPERTS, SPLIT, up_all.shape[1], up_all.shape[2])
    down_set = down_all.reshape(EXPERTS, SPLIT, down_all.shape[1], down_all.shape[2])
    return (gate_set, up_set, down_set)

def forward_rank(inputs, expert_ids, gain_row, router_cols, gate_all, up_all, down_all):
    normed, values, inverse = normalize(inputs, gain_row)
    scores, share, picker = route_gates(normed, router_cols, expert_ids)
    flat_ids = expert_ids.reshape(-1)
    flat_share = share.reshape(-1)
    capacity_rows = N_EXPERT * CAP
    gate_set, up_set, down_set = split_weights(gate_all, up_all, down_all)

    def one_expert(branch, packed):
        gate_w, up_w, down_w, number = packed
        matches = flat_ids == number
        picked = jnp.nonzero(matches, size=capacity_rows, fill_value=0)[0]
        is_valid = (jnp.arange(capacity_rows) < jnp.sum(matches))[:, None]
        token_rows = picked // TOP
        rows_in = normed[token_rows]
        total = jnp.zeros((capacity_rows, values.shape[1]), jnp.float32)
        for slice_index in range(SPLIT):
            part = expert_forward(rows_in, gate_w[slice_index], up_w[slice_index], down_w[slice_index])[0]
            total = total + part.astype(jnp.float32)
        weighted = jnp.where(is_valid, flat_share[picked][:, None] * total, 0.0)
        return (branch.at[token_rows].add(weighted), None)
    numbers = jnp.arange(EXPERTS, dtype=jnp.int32)
    branch = lax.scan(one_expert, jnp.zeros(values.shape, jnp.float32), (gate_set, up_set, down_set, numbers))[0]
    return (values + route_scale * branch).astype(jnp.bfloat16)

def backward_rank(inputs, grad_out, expert_ids, gain_row, router_cols, gate_all, up_all, down_all):
    normed, values, inverse = normalize(inputs, gain_row)
    scores, share, picker = route_gates(normed, router_cols, expert_ids)
    flat_ids = expert_ids.reshape(-1)
    flat_share = share.reshape(-1)
    capacity_rows = N_EXPERT * CAP
    gate_set, up_set, down_set = split_weights(gate_all, up_all, down_all)

    def one_expert(running, packed):
        branch, contracts = running
        gate_w, up_w, down_w, number = packed
        matches = flat_ids == number
        picked = jnp.nonzero(matches, size=capacity_rows, fill_value=0)[0]
        is_valid = jnp.arange(capacity_rows) < jnp.sum(matches)
        token_rows = picked // TOP
        rows_in = normed[token_rows]
        rows_grad = grad_out[token_rows]
        grad_total = jnp.zeros((capacity_rows, values.shape[1]), jnp.float32)
        contract_total = jnp.zeros((capacity_rows,), jnp.float32)
        for slice_index in range(SPLIT):
            grad_in, contract = expert_backward(rows_in, rows_grad, gate_w[slice_index], up_w[slice_index], down_w[slice_index])
            grad_total = grad_total + grad_in.astype(jnp.float32)
            contract_total = contract_total + contract.astype(jnp.float32)
        weighted = jnp.where(is_valid[:, None], flat_share[picked][:, None] * grad_total, 0.0)
        contracts = contracts.at[picked].add(jnp.where(is_valid, contract_total, 0.0))
        return ((branch.at[token_rows].add(weighted), contracts), None)
    numbers = jnp.arange(EXPERTS, dtype=jnp.int32)
    start = (jnp.zeros(values.shape, jnp.float32), jnp.zeros(flat_ids.shape, jnp.float32))
    branch, contracts = lax.scan(one_expert, start, (gate_set, up_set, down_set, numbers))[0]
    grad_share = route_scale * contracts.reshape(share.shape)
    grad_scores = (grad_share - lax.optimization_barrier(jnp.sum(share * grad_share, axis=1, keepdims=True))) / lax.optimization_barrier(jnp.sum(scores, axis=1, keepdims=True))
    grad_logit = grad_scores * scores * (1.0 - scores)
    dense_grad = lax.optimization_barrier(jnp.sum(jnp.where(picker, grad_logit[:, :, None], 0.0), axis=1)).astype(jnp.bfloat16)
    router_term = lax.dot_general(dense_grad, router_cols, (((1,), (1,)), ((), ())), preferred_element_type=jnp.float32)
    grad_normed = (route_scale * branch + router_term) * gain_row.astype(jnp.float32)
    center = lax.optimization_barrier(jnp.mean(values * grad_normed, axis=-1, keepdims=True))
    grad_values = grad_out.astype(jnp.float32) + inverse * grad_normed - values * inverse * inverse * inverse * center
    return grad_values.astype(jnp.bfloat16)

def reference(act_a, ids_a, act_b, cot_b, ids_b, norm_gain, router, w_gate, w_up, w_down):
    forward_all = []
    backward_all = []
    for section_index in range(N_PIPE):
        forward_all.append(forward_rank(act_a[section_index], ids_a[section_index], norm_gain[section_index], router[section_index], w_gate[section_index], w_up[section_index], w_down[section_index]))
        backward_all.append(backward_rank(act_b[section_index], cot_b[section_index], ids_b[section_index], norm_gain[section_index], router[section_index], w_gate[section_index], w_up[section_index], w_down[section_index]))
    next_a = jnp.roll(jnp.stack(forward_all), 1, axis=0)
    next_b = jnp.roll(jnp.stack(backward_all), -1, axis=0)
    return (next_a, next_b)
```

```python
import jax
import jax.numpy as jnp
from jax import lax
from jax.sharding import PartitionSpec as P

SPLIT = 4


route_scale = 2.5
norm_eps = 1e-06
last_dims = (((1,), (1,)), ((), ()))


def dot(left, right):
    return jnp.dot(left, right, preferred_element_type=jnp.float32)


def dot_last(left, right):
    return lax.dot_general(left, right, last_dims, preferred_element_type=jnp.float32)


def from_behind(array, axis, by):
    size = lax.axis_size(axis)
    return lax.ppermute(array, axis, [(i, (i + by) % size) for i in range(size)])


def from_partner(array, bit):
    size = lax.axis_size("expert")
    return lax.ppermute(array, "expert", [(i, i ^ bit) for i in range(size)])


def normalize(inputs, gain_row):
    values = inputs.astype(jnp.float32)
    inverse = lax.rsqrt(jnp.mean(values * values, axis=-1, keepdims=True) + norm_eps)
    normed = (values * inverse * gain_row.astype(jnp.float32)).astype(jnp.bfloat16)
    return (normed, values, inverse)


def route_gates(normed, router_cols, expert_ids):
    logits = dot(normed, router_cols)
    picker = (
        expert_ids[:, :, None] == jnp.arange(router_cols.shape[1], dtype=jnp.int32)[None, None, :]
    )
    chosen = jnp.sum(jnp.where(picker, logits[:, None, :], 0.0), axis=2)
    scores = jax.nn.sigmoid(chosen)
    return (scores, scores / jnp.sum(scores, axis=1, keepdims=True), picker)


def slot_masks(picker, capacity):
    tokens, _, experts = picker.shape
    named = jnp.any(picker, axis=1)
    below = jnp.tril(jnp.ones((tokens, tokens), jnp.bfloat16))
    place = dot(below, named.astype(jnp.bfloat16)).astype(jnp.int32) - 1
    slots = jnp.arange(capacity, dtype=jnp.int32)
    chosen = (place[:, :, None] == slots[None, None, :]) & named[:, :, None]
    by_rank = picker[:, :, :, None] & chosen[:, None]
    pack = chosen.reshape(tokens, experts * capacity).astype(jnp.bfloat16)
    unpack = by_rank.reshape(tokens, picker.shape[1], experts * capacity).astype(jnp.bfloat16)
    return (pack, unpack)


def pack_rows(pack, source, experts):
    packed = lax.dot_general(
        pack, source, (((0,), (0,)), ((), ())), preferred_element_type=jnp.float32
    ).astype(jnp.bfloat16)
    return packed.reshape(experts, -1, source.shape[1])


def swap_experts(blocks):
    size = lax.axis_size("expert")
    experts = size // SPLIT
    mine = lax.axis_index("expert") // SPLIT
    parts = [lax.dynamic_index_in_dim(blocks, mine, 0, keepdims=False)]
    for step in range(1, experts):
        block = lax.dynamic_index_in_dim(blocks, (mine + step) % experts, 0, keepdims=False)
        pairs = [(i, (i + step * SPLIT) % size) for i in range(size)]
        parts.append(lax.ppermute(block, "expert", pairs))
    return parts


def return_experts(parts):
    size = lax.axis_size("expert")
    experts = size // SPLIT
    mine = lax.axis_index("expert") // SPLIT
    home = [parts[0]]
    for step in range(1, experts):
        pairs = [(i, (i - step * SPLIT) % size) for i in range(size)]
        home.append(lax.ppermute(parts[step], "expert", pairs))
    stacked = jnp.stack(home)
    return jnp.roll(stacked, mine, axis=0)


def forward_slice(rows, gate_w, up_w):
    gate_pre = dot(rows, gate_w)
    up_pre = dot(rows, up_w)
    sig_gate = jax.nn.sigmoid(gate_pre)
    activation = (gate_pre * sig_gate * up_pre).astype(jnp.bfloat16)
    return (activation, gate_pre, up_pre, sig_gate)


def backward_slice(rows, grad_rows, gate_w, up_w, down_w):
    activation, gate_pre, up_pre, sig_gate = forward_slice(rows, gate_w, up_w)
    grad_act = dot_last(grad_rows, down_w)
    contract = jnp.sum(activation.astype(jnp.float32) * grad_act, axis=-1, keepdims=True)
    grad_gate = (grad_act * up_pre * sig_gate * (1.0 + gate_pre * (1.0 - sig_gate))).astype(
        jnp.bfloat16
    )
    grad_up = (grad_act * gate_pre * sig_gate).astype(jnp.bfloat16)
    return (dot_last(grad_gate, gate_w) + dot_last(grad_up, up_w), contract)


def per_device(act_a, ids_a, act_b, cot_b, ids_b, norm_gain, router, w_gate, w_up, w_down):
    experts = lax.axis_size("expert") // SPLIT
    token_count = act_a.shape[1]
    top_count = ids_a.shape[2]
    width = act_a.shape[2]
    capacity = min(token_count, max(2, 5 * token_count * top_count // (4 * experts)))
    gain_row = norm_gain[0]
    router_cols = router[0]
    own = (w_gate[0, 0], w_up[0, 0], w_down[0, 0])
    other = tuple(from_partner(w, 1) for w in own)

    normed_a, values_a, inverse_a = normalize(act_a[0], gain_row)
    scores_a, share_a, picker_a = route_gates(normed_a, router_cols, ids_a[0])
    pack_a, unpack_a = slot_masks(picker_a, capacity)
    parts_a = swap_experts(pack_rows(pack_a, normed_a, experts))

    grad_out = cot_b[0]
    normed_b, values_b, inverse_b = normalize(act_b[0], gain_row)
    scores_b, share_b, picker_b = route_gates(normed_b, router_cols, ids_b[0])
    pack_b, unpack_b = slot_masks(picker_b, capacity)
    both_b = jnp.concatenate(
        [pack_rows(pack_b, normed_b, experts), pack_rows(pack_b, grad_out, experts)], axis=1
    )
    parts_b = swap_experts(both_b)

    rows_a = jnp.concatenate(parts_a)
    far_a = from_partner(rows_a, 2)
    rows_b = jnp.concatenate([part[:capacity] for part in parts_b])
    cots_b = jnp.concatenate([part[capacity:] for part in parts_b])
    far_b = from_partner(rows_b, 2)
    far_cots = from_partner(cots_b, 2)

    def forward(rows):
        act_own = forward_slice(rows, own[0], own[1])[0]
        act_other = forward_slice(rows, other[0], other[1])[0]
        return dot(act_own, own[2]) + dot(act_other, other[2])

    def backward(rows, cots):
        first, first_c = backward_slice(rows, cots, *own)
        second, second_c = backward_slice(rows, cots, *other)
        return (first + second, first_c + second_c)

    back_a = from_partner(forward(far_a).astype(jnp.bfloat16), 2)
    out_a = (forward(rows_a) + back_a.astype(jnp.float32)).astype(jnp.bfloat16)
    home_a = return_experts(list(out_a.reshape(experts, capacity, width)))

    far_grad, far_contract = backward(far_b, far_cots)
    back_grad = from_partner(far_grad.astype(jnp.bfloat16), 2)
    back_contract = from_partner(
        jnp.broadcast_to(far_contract, (experts * capacity, 128)).astype(jnp.bfloat16), 2
    )
    near_grad, near_contract = backward(rows_b, cots_b)
    out_grad = (near_grad + back_grad.astype(jnp.float32)).astype(jnp.bfloat16)
    out_contract = (near_contract + back_contract.astype(jnp.float32)).astype(jnp.bfloat16)
    home_grad = return_experts(list(out_grad.reshape(experts, capacity, width)))
    home_contract = return_experts(list(out_contract.reshape(experts, capacity, 128)))

    home_a = home_a.reshape(-1, width)
    mixed_a = sum(share_a[:, k : k + 1] * dot(unpack_a[:, k], home_a) for k in range(top_count))
    section_a = (values_a + route_scale * mixed_a).astype(jnp.bfloat16)
    next_a = from_behind(section_a[None], "pipe", 1)

    home_grad = home_grad.reshape(-1, width)
    home_contract = home_contract.reshape(-1, 128)
    branch_b = sum(share_b[:, k : k + 1] * dot(unpack_b[:, k], home_grad) for k in range(top_count))
    contracts = jnp.concatenate(
        [dot(unpack_b[:, k], home_contract)[:, :1] for k in range(top_count)], axis=1
    )
    grad_share = route_scale * contracts
    grad_scores = (grad_share - jnp.sum(share_b * grad_share, axis=1, keepdims=True)) / jnp.sum(
        scores_b, axis=1, keepdims=True
    )
    grad_logit = grad_scores * scores_b * (1.0 - scores_b)
    dense_grad = jnp.sum(jnp.where(picker_b, grad_logit[:, :, None], 0.0), axis=1).astype(
        jnp.bfloat16
    )
    router_term = dot_last(dense_grad, router_cols)
    grad_normed = (route_scale * branch_b + router_term) * gain_row.astype(jnp.float32)
    center = jnp.mean(values_b * grad_normed, axis=-1, keepdims=True)
    grad_values = (
        grad_out.astype(jnp.float32)
        + inverse_b * grad_normed
        - values_b * inverse_b * inverse_b * inverse_b * center
    )
    next_b = from_behind(grad_values.astype(jnp.bfloat16)[None], "pipe", -1)
    return (next_a, next_b)


def solution(mesh):
    return jax.shard_map(
        per_device,
        mesh=mesh,
        in_specs=(
            P("pipe", "expert", None),
            P("pipe", "expert", None),
            P("pipe", "expert", None),
            P("pipe", "expert", None),
            P("pipe", "expert", None),
            P("pipe", None),
            P("pipe", None, None),
            P("pipe", "expert", None, None),
            P("pipe", "expert", None, None),
            P("pipe", "expert", None, None),
        ),
        out_specs=(P("pipe", "expert", None), P("pipe", "expert", None)),
        check_vma=False,
    )
```

```python
import functools
import jax
import jax.numpy as jnp
from jax import lax
from jax.experimental import pallas as pl
from jax.experimental.pallas import tpu as pltpu
from jax.sharding import PartitionSpec as P

SPLIT = 4
CHUNKS = 4
LANES = 128
MESH = pl.DeviceIdType.MESH

route_scale = 2.5
norm_eps = 1e-06
last_dims = (((1,), (1,)), ((), ()))


def dot(left, right):
    return jnp.dot(left, right, preferred_element_type=jnp.float32)


def dot_last(left, right):
    return lax.dot_general(left, right, last_dims, preferred_element_type=jnp.float32)


def kernel(
    sizes,
    act_a,
    ids_a,
    idst_a,
    act_b,
    cot_b,
    ids_b,
    idst_b,
    gain,
    router,
    w_gate,
    w_up,
    w_down,
    next_a,
    next_b,
    own_g,
    own_u,
    own_d,
    oth_g,
    oth_u,
    oth_d,
    normed,
    send_a,
    send_b,
    send_c,
    rows_a,
    rows_b,
    rows_c,
    gate_s,
    up_s,
    gact_s,
    mid_a,
    mid_g,
    mid_u,
    near_a,
    near_b,
    ysend_a,
    ysend_b,
    ysend_c,
    yback_a,
    yback_b,
    yback_c,
    zsend_a,
    zsend_b,
    zsend_c,
    home_a,
    home_b,
    home_c,
    grad_n,
    sect_a,
    sect_b,
    load_sem,
    w_send,
    w_recv,
    z_send,
    z_recv,
    y_send,
    y_recv,
    yb_send,
    yb_recv,
    zb_send,
    zb_recv,
    p_send,
    p_recv,
):
    n_expert, n_pipe, experts, slot, top, width, hidden, tokens = sizes
    total_slots = experts * slot
    rows = 2 * total_slots
    cut = width // CHUNKS
    me = lax.axis_index("expert")
    pipe = lax.axis_index("pipe")
    mine = me // SPLIT
    x_dev = {"expert": me + 1 - 2 * (me % 2)}
    y_dev = {"expert": me + 2 - 4 * ((me // 2) % 2)}

    def ahead(step):
        return {"expert": (me + SPLIT * step) % n_expert}

    def behind(step):
        return {"expert": (me + n_expert - SPLIT * step) % n_expert}

    next_pipe = {"pipe": (pipe + 1) % n_pipe}
    last_pipe = {"pipe": (pipe + n_pipe - 1) % n_pipe}

    def remote(src, dst, send, recv, device):
        return pltpu.make_async_remote_copy(
            src_ref=src,
            dst_ref=dst,
            send_sem=send,
            recv_sem=recv,
            device_id=device,
            device_id_type=MESH,
        )

    def columns(n):
        if isinstance(n, int):
            return pl.ds(n * cut, cut)
        return pl.ds(pl.multiple_of(n * cut, cut), cut)

    loads = [
        pltpu.make_async_copy(src, dst, load_sem.at[i])
        for i, (src, dst) in enumerate(((w_gate, own_g), (w_up, own_u), (w_down, own_d)))
    ]
    for load in loads:
        load.start()

    partners = [x_dev, y_dev] + [ahead(step) for step in range(1, experts)] + [next_pipe]
    if n_pipe > 2:
        partners.append(last_pipe)
    barrier = pltpu.get_barrier_semaphore()
    for partner in partners:
        pl.semaphore_signal(barrier, inc=1, device_id=partner, device_id_type=MESH)
    pl.semaphore_wait(barrier, len(partners))

    w_copies = [
        remote(w_gate, oth_g, w_send.at[0], w_recv.at[0], x_dev),
        remote(w_up, oth_u, w_send.at[1], w_recv.at[1], x_dev),
    ]

    def down_copy(n):
        cols = columns(n)
        return remote(
            w_down.at[:, cols], oth_d.at[:, cols], w_send.at[2 + n], w_recv.at[2 + n], x_dev
        )

    for copy in w_copies:
        copy.start()
    for n in range(CHUNKS):
        down_copy(n).start()

    def z_copy(i, send, into, step):
        return remote(
            send.at[step], into.at[0, step], z_send.at[i, step], z_recv.at[i, step], ahead(step)
        )

    def y_copy(i, into, step):
        return remote(
            into.at[0, step], into.at[1, step], y_send.at[i, step], y_recv.at[i, step], y_dev
        )

    def block_of(index):
        count = jnp.zeros_like(index)
        for step in range(1, experts):
            count = count + jnp.where(index >= step * slot, 1, 0)
        place = (index - count * slot).astype(jnp.float32)
        expert = count + mine
        return jnp.where(expert >= experts, expert - experts, expert), place

    gain_row = gain[...].astype(jnp.float32)

    def normalize(act):
        values = act[...].astype(jnp.float32)
        inverse = lax.rsqrt(jnp.mean(values * values, axis=-1, keepdims=True) + norm_eps)
        normed[...] = (values * inverse * gain_row).astype(jnp.bfloat16)
        return inverse

    def route(ids):
        logits = dot_last(normed[...], router[...])
        number = lax.broadcasted_iota(jnp.int32, logits.shape, 1)
        scores = [
            jax.nn.sigmoid(
                jnp.sum(
                    jnp.where(ids[:, k : k + 1] == number, logits, 0.0), axis=1, keepdims=True
                )
            )
            for k in range(top)
        ]
        whole = functools.reduce(lambda a, b: a + b, scores)
        return scores, [score / whole for score in scores], whole

    def pack_mask(idst):
        expert, place = block_of(lax.broadcasted_iota(jnp.int32, (total_slots, tokens), 0))
        named = jnp.zeros((total_slots, tokens), jnp.float32)
        for k in range(top):
            named = named + jnp.where(idst[k : k + 1, :] == expert, 1.0, 0.0)
        first = lax.broadcasted_iota(jnp.int32, (tokens, tokens), 0)
        second = lax.broadcasted_iota(jnp.int32, (tokens, tokens), 1)
        upper = jnp.where(first <= second, 1.0, 0.0).astype(jnp.bfloat16)
        count = dot(named.astype(jnp.bfloat16), upper)
        return jnp.where(count - 1.0 == place, named, 0.0).astype(jnp.bfloat16)

    def unpack_masks(ids):
        expert, place = block_of(lax.broadcasted_iota(jnp.int32, (tokens, total_slots), 1))
        hits = [jnp.where(ids[:, k : k + 1] == expert, 1.0, 0.0) for k in range(top)]
        named = functools.reduce(lambda a, b: a + b, hits)
        first = lax.broadcasted_iota(jnp.int32, (tokens, tokens), 0)
        second = lax.broadcasted_iota(jnp.int32, (tokens, tokens), 1)
        lower = jnp.where(second <= first, 1.0, 0.0).astype(jnp.bfloat16)
        count = dot(lower, named.astype(jnp.bfloat16))
        return [jnp.where(count - 1.0 == place, hit, 0.0).astype(jnp.bfloat16) for hit in hits]

    def pack(i, mask, source, send, into):
        def body(n, carry):
            cols = columns(n)
            packed = dot(mask, source[:, cols]).reshape(experts, slot, cut).astype(jnp.bfloat16)
            send[:, :, cols] = packed
            into[0, 0, :, cols] = packed[0]
            return carry

        lax.fori_loop(0, CHUNKS, body, 0)
        for step in range(1, experts):
            z_copy(i, send, into, step).start()
        y_copy(i, into, 0).start()

    def forward_blocks(i, send, into):
        for step in range(1, experts):
            z_copy(i, send, into, step).wait_recv()
            y_copy(i, into, step).start()

    def arrived(i, into):
        for step in range(experts):
            y_copy(i, into, step).wait_recv()

    inverse_a = normalize(act_a)
    share_a = route(ids_a)[1]
    pack(0, pack_mask(idst_a), normed, send_a, rows_a)
    inverse_b = normalize(act_b)
    mask_b = pack_mask(idst_b)
    pack(1, mask_b, normed, send_b, rows_b)
    pack(2, mask_b, cot_b, send_c, rows_c)
    scores_b, share_b, whole_b = route(ids_b)

    def project(into, gate_w, up_w, half):
        lanes = pl.ds(half * hidden, hidden)

        def body(n, carry):
            cols = columns(n)
            part = into[:, :, :, cols].reshape(rows, cut)
            gate = dot(part, gate_w[cols, :])
            up = dot(part, up_w[cols, :])

            @pl.when(n == 0)
            def _():
                gate_s[:, lanes] = gate
                up_s[:, lanes] = up

            @pl.when(n > 0)
            def _():
                gate_s[:, lanes] += gate
                up_s[:, lanes] += up

            return carry

        lax.fori_loop(0, CHUNKS, body, 0)

    def grad_hidden(n, down_w, half):
        lanes = pl.ds(half * hidden, hidden)
        cols = columns(n)
        part = rows_c[:, :, :, cols].reshape(rows, cut)
        gact_s[:, lanes] += dot_last(part, down_w[:, cols])

    def activate(half):
        lanes = pl.ds(half * hidden, hidden)
        gate = gate_s[:, lanes]
        mid_a[:, lanes] = (gate * jax.nn.sigmoid(gate) * up_s[:, lanes]).astype(jnp.bfloat16)

    forward_blocks(0, send_a, rows_a)
    for load in loads:
        load.wait()
    forward_blocks(1, send_b, rows_b)
    arrived(0, rows_a)
    project(rows_a, own_g, own_u, 0)
    activate(0)
    forward_blocks(2, send_c, rows_c)
    arrived(1, rows_b)
    project(rows_b, own_g, own_u, 0)
    gact_s[...] = jnp.zeros_like(gact_s)
    arrived(2, rows_c)

    def own_grad(n, carry):
        grad_hidden(n, own_d, 0)
        return carry

    lax.fori_loop(0, CHUNKS, own_grad, 0)

    for copy in w_copies:
        copy.wait_recv()
    project(rows_a, oth_g, oth_u, 1)
    activate(1)
    project(rows_b, oth_g, oth_u, 1)

    def yb_copy(i, n, source, into):
        cols = columns(n)
        return remote(
            source.at[:, :, cols], into.at[:, :, cols], yb_send.at[i, n], yb_recv.at[i, n], y_dev
        )

    def zb_copy(i, n, source, into, step):
        cols = columns(n)
        return remote(
            source.at[step, :, cols],
            into.at[step, :, cols],
            zb_send.at[i, n, step],
            zb_recv.at[i, n, step],
            behind(step),
        )

    def split_out(i, n, out, near, source, into):
        cols = columns(n)
        near[:, cols] = out[:total_slots]
        far = out[total_slots:].reshape(experts, slot, cut)
        source[:, :, cols] = far.astype(jnp.bfloat16)
        yb_copy(i, n, source, into).start()

    def join(i, n, near, ysource, yinto, zsource, zinto):
        cols = columns(n)
        yb_copy(i, n, ysource, yinto).wait_recv()
        summed = near[:, cols].reshape(experts, slot, cut) + yinto[:, :, cols].astype(jnp.float32)
        summed = summed.astype(jnp.bfloat16)
        zsource[:, :, cols] = summed
        zinto[0, :, cols] = summed[0]
        for step in range(1, experts):
            zb_copy(i, n, zsource, zinto, step).start()

    def down_step(n):
        cols = columns(n)
        down_copy(n).wait_recv()
        out = dot(mid_a[:, :hidden], own_d[:, cols]) + dot(mid_a[:, hidden:], oth_d[:, cols])
        split_out(0, n, out, near_a, ysend_a, yback_a)
        grad_hidden(n, oth_d, 1)

    def join_a(n):
        join(0, n, near_a, ysend_a, yback_a, zsend_a, home_a)

    def down_loop(n, carry):
        down_step(n)
        join_a(n - 1)
        return carry

    down_step(0)
    lax.fori_loop(1, CHUNKS, down_loop, 0)

    gate = gate_s[...]
    sig = jax.nn.sigmoid(gate)
    up = up_s[...]
    gact = gact_s[...]
    swish = gate * sig
    mid_g[...] = (gact * up * sig * (1.0 + gate * (1.0 - sig))).astype(jnp.bfloat16)
    mid_u[...] = (gact * swish).astype(jnp.bfloat16)
    active = (swish * up).astype(jnp.bfloat16).astype(jnp.float32)
    contract = jnp.broadcast_to(
        jnp.sum(active * gact, axis=-1, keepdims=True), (rows, LANES)
    )
    ysend_c[...] = contract[total_slots:].reshape(experts, slot, LANES).astype(jnp.bfloat16)
    near_c = contract[:total_slots].reshape(experts, slot, LANES)
    yc_copy = remote(ysend_c, yback_c, yb_send.at[1, CHUNKS], yb_recv.at[1, CHUNKS], y_dev)
    yc_copy.start()

    def zc_copy(step):
        return remote(
            zsend_c.at[step],
            home_c.at[step],
            zb_send.at[1, CHUNKS, step],
            zb_recv.at[1, CHUNKS, step],
            behind(step),
        )

    def grad_step(n):
        cols = columns(n)
        out = dot_last(mid_g[:, :hidden], own_g[cols, :])
        out = out + dot_last(mid_u[:, :hidden], own_u[cols, :])
        out = out + dot_last(mid_g[:, hidden:], oth_g[cols, :])
        out = out + dot_last(mid_u[:, hidden:], oth_u[cols, :])
        split_out(1, n, out, near_b, ysend_b, yback_b)

    def join_b(n):
        join(1, n, near_b, ysend_b, yback_b, zsend_b, home_b)

    grad_step(0)
    join_a(CHUNKS - 1)
    yc_copy.wait_recv()
    summed_c = (near_c + yback_c[...].astype(jnp.float32)).astype(jnp.bfloat16)
    zsend_c[...] = summed_c
    home_c[0] = summed_c[0]
    for step in range(1, experts):
        zc_copy(step).start()

    def grad_loop(n, carry):
        grad_step(n)
        join_b(n - 1)
        return carry

    lax.fori_loop(1, CHUNKS, grad_loop, 0)
    join_b(CHUNKS - 1)

    def mix(i, n, zsource, zinto, masks, share):
        cols = columns(n)
        for step in range(1, experts):
            zb_copy(i, n, zsource, zinto, step).wait_recv()
        block = zinto[:, :, cols].reshape(total_slots, cut)
        return functools.reduce(
            lambda a, b: a + b, [share[k] * dot(masks[k], block) for k in range(top)]
        )

    masks_a = unpack_masks(ids_a)

    def finish_a(n, carry):
        cols = columns(n)
        mixed = mix(0, n, zsend_a, home_a, masks_a, share_a)
        values = act_a[:, cols].astype(jnp.float32)
        sect_a[:, cols] = (values + route_scale * mixed).astype(jnp.bfloat16)
        return carry

    lax.fori_loop(0, CHUNKS, finish_a, 0)
    pa_copy = remote(sect_a, next_a, p_send.at[0], p_recv.at[0], next_pipe)
    pa_copy.start()

    masks_b = unpack_masks(ids_b)
    for step in range(1, experts):
        zc_copy(step).wait_recv()
    home = home_c[...].reshape(total_slots, LANES)
    grad_share = [route_scale * dot(masks_b[k], home)[:, :1] for k in range(top)]
    center = functools.reduce(
        lambda a, b: a + b, [share_b[k] * grad_share[k] for k in range(top)]
    )
    number = lax.broadcasted_iota(jnp.int32, (tokens, router.shape[0]), 1)
    dense = jnp.zeros((tokens, router.shape[0]), jnp.float32)
    for k in range(top):
        grad_score = (grad_share[k] - center) / whole_b
        grad_logit = grad_score * scores_b[k] * (1.0 - scores_b[k])
        dense = dense + jnp.where(ids_b[:, k : k + 1] == number, grad_logit, 0.0)
    dense = dense.astype(jnp.bfloat16)

    def finish_b(n, inner):
        cols = columns(n)
        branch = mix(1, n, zsend_b, home_b, masks_b, share_b)
        term = dot(dense, router[:, cols])
        grad = (route_scale * branch + term) * gain[:, cols].astype(jnp.float32)
        grad_n[:, cols] = grad
        values = act_b[:, cols].astype(jnp.float32)
        return inner + jnp.sum(values * grad, axis=-1, keepdims=True)

    inner = lax.fori_loop(0, CHUNKS, finish_b, jnp.zeros((tokens, 1), jnp.float32))
    scale = inverse_b * inverse_b * inverse_b * (inner / width)

    def write_b(n, carry):
        cols = columns(n)
        values = act_b[:, cols].astype(jnp.float32)
        out = cot_b[:, cols].astype(jnp.float32) + inverse_b * grad_n[:, cols] - values * scale
        sect_b[:, cols] = out.astype(jnp.bfloat16)
        return carry

    lax.fori_loop(0, CHUNKS, write_b, 0)
    pb_copy = remote(sect_b, next_b, p_send.at[1], p_recv.at[1], last_pipe)
    pb_copy.start()

    for copy in w_copies:
        copy.wait_send()
    for i, (send, into) in enumerate(((send_a, rows_a), (send_b, rows_b), (send_c, rows_c))):
        y_copy(i, into, 0).wait_send()
        for step in range(1, experts):
            z_copy(i, send, into, step).wait_send()
            y_copy(i, into, step).wait_send()

    def drain(n, carry):
        down_copy(n).wait_send()
        yb_copy(0, n, ysend_a, yback_a).wait_send()
        yb_copy(1, n, ysend_b, yback_b).wait_send()
        for step in range(1, experts):
            zb_copy(0, n, zsend_a, home_a, step).wait_send()
            zb_copy(1, n, zsend_b, home_b, step).wait_send()
        return carry

    lax.fori_loop(0, CHUNKS, drain, 0)
    yc_copy.wait_send()
    for step in range(1, experts):
        zc_copy(step).wait_send()
    pa_copy.wait()
    pb_copy.wait()


def per_device(act_a, ids_a, act_b, cot_b, ids_b, norm_gain, router, w_gate, w_up, w_down):
    n_expert = lax.axis_size("expert")
    n_pipe = lax.axis_size("pipe")
    experts = n_expert // SPLIT
    tokens, width = act_a.shape[1:]
    top = ids_a.shape[2]
    hidden = w_gate.shape[3]
    capacity = min(tokens, max(2, 5 * tokens * top // (4 * experts)))
    slot = -(-capacity // SLOT_ROWS) * SLOT_ROWS
    slots = experts * slot
    rows = 2 * slots
    router_rows = jnp.pad(router[0].T, ((0, max(0, 16 - experts)), (0, 0)))
    sizes = (n_expert, n_pipe, experts, slot, top, width, hidden, tokens)

    def half(*dims):
        return pltpu.VMEM(dims, jnp.bfloat16)

    def full(*dims):
        return pltpu.VMEM(dims, jnp.float32)

    sem = pltpu.SemaphoreType.DMA
    block = (experts, slot, width)
    narrow = (experts, slot, LANES)
    vmem = pl.BlockSpec(memory_space=pltpu.VMEM)
    anywhere = pl.BlockSpec(memory_space=pl.ANY)
    out = jax.ShapeDtypeStruct((tokens, width), jnp.bfloat16)
    next_a, next_b = pl.pallas_call(
        functools.partial(kernel, sizes),
        out_shape=(out, out),
        in_specs=[vmem] * 9 + [anywhere] * 3,
        out_specs=(anywhere, anywhere),
        scratch_shapes=[
            half(width, hidden),
            half(width, hidden),
            half(hidden, width),
            half(width, hidden),
            half(width, hidden),
            half(hidden, width),
            half(tokens, width),
            half(*block),
            half(*block),
            half(*block),
            half(2, *block),
            half(2, *block),
            half(2, *block),
            full(rows, 2 * hidden),
            full(rows, 2 * hidden),
            full(rows, 2 * hidden),
            half(rows, 2 * hidden),
            half(rows, 2 * hidden),
            half(rows, 2 * hidden),
            full(slots, width),
            full(slots, width),
            half(*block),
            half(*block),
            half(*narrow),
            half(*block),
            half(*block),
            half(*narrow),
            half(*block),
            half(*block),
            half(*narrow),
            half(*block),
            half(*block),
            half(*narrow),
            full(tokens, width),
            half(tokens, width),
            half(tokens, width),
            sem((3,)),
            sem((2 + CHUNKS,)),
            sem((2 + CHUNKS,)),
            sem((3, experts)),
            sem((3, experts)),
            sem((3, experts)),
            sem((3, experts)),
            sem((2, CHUNKS + 1)),
            sem((2, CHUNKS + 1)),
            sem((2, CHUNKS + 1, experts)),
            sem((2, CHUNKS + 1, experts)),
            sem((2,)),
            sem((2,)),
        ],
        compiler_params=pltpu.CompilerParams(
            collective_id=0, has_side_effects=True, vmem_limit_bytes=60 * 1024 * 1024
        ),
        cost_estimate=pl.CostEstimate(
            flops=2 * 9 * rows * width * hidden * 2,
            bytes_accessed=6 * width * hidden * 2,
            transcendentals=0,
        ),
    )(
        act_a[0],
        ids_a[0],
        ids_a[0].T,
        act_b[0],
        cot_b[0],
        ids_b[0],
        ids_b[0].T,
        norm_gain,
        router_rows,
        w_gate[0, 0],
        w_up[0, 0],
        w_down[0, 0],
    )
    return (next_a[None], next_b[None])


SLOT_ROWS = 8


def solution(mesh):
    return jax.shard_map(
        per_device,
        mesh=mesh,
        in_specs=(
            P("pipe", "expert", None),
            P("pipe", "expert", None),
            P("pipe", "expert", None),
            P("pipe", "expert", None),
            P("pipe", "expert", None),
            P("pipe", None),
            P("pipe", None, None),
            P("pipe", "expert", None, None),
            P("pipe", "expert", None, None),
            P("pipe", "expert", None, None),
        ),
        out_specs=(P("pipe", "expert", None), P("pipe", "expert", None)),
        check_vma=False,
    )
```

```python
import functools
import jax
import jax.numpy as jnp
from jax import lax
from jax.experimental import pallas as pl
from jax.experimental.pallas import tpu as pltpu
from jax.sharding import PartitionSpec as P

SPLIT = 4
CHUNKS = 7
LANES = 128
MESH = pl.DeviceIdType.MESH

route_scale = 2.5
norm_eps = 1e-06
last_dims = (((1,), (1,)), ((), ()))


def dot(left, right):
    return jnp.dot(left, right, preferred_element_type=jnp.float32)


def dot_last(left, right):
    return lax.dot_general(left, right, last_dims, preferred_element_type=jnp.float32)


def kernel(
    sizes,
    act_a_hbm,
    act_b_hbm,
    cot_b_hbm,
    idst_a,
    idst_b,
    gain,
    router,
    w_gate,
    w_up,
    w_down,
    next_a,
    next_b,
    own_g,
    own_u,
    own_d,
    oth_g,
    oth_u,
    oth_d,
    act_a,
    act_b,
    cot_b,
    normed,
    send_a,
    send_b,
    send_c,
    rows_a,
    rows_b,
    rows_c,
    gate_s,
    up_s,
    gact_s,
    mid_a,
    mid_g,
    mid_u,
    mid_x,
    near_a,
    part_b,
    ysend_a,
    ysend_b,
    ysend_c,
    yback_a,
    yback_b,
    yback_c,
    zsend_c,
    home_a,
    home_b,
    home_c,
    grad_n,
    sect_a,
    sect_b,
    load_sem,
    w_send,
    w_recv,
    z_send,
    z_recv,
    y_send,
    y_recv,
    yb_send,
    yb_recv,
    zb_send,
    zb_recv,
    p_send,
    p_recv,
):
    n_expert, n_pipe, experts, slot, top, width, hidden, tokens = sizes
    total_slots = experts * slot
    rows = 2 * total_slots
    cut = width // CHUNKS
    me = lax.axis_index("expert")
    pipe = lax.axis_index("pipe")
    mine = me // SPLIT
    x_dev = {"expert": me + 1 - 2 * (me % 2)}
    y_dev = {"expert": me + 2 - 4 * ((me // 2) % 2)}

    def ahead(step):
        return {"expert": (me + SPLIT * step) % n_expert}

    def behind(step):
        return {"expert": (me + n_expert - SPLIT * step) % n_expert}

    next_pipe = {"pipe": (pipe + 1) % n_pipe}
    last_pipe = {"pipe": (pipe + n_pipe - 1) % n_pipe}

    def remote(src, dst, send, recv, device):
        return pltpu.make_async_remote_copy(
            src_ref=src,
            dst_ref=dst,
            send_sem=send,
            recv_sem=recv,
            device_id=device,
            device_id_type=MESH,
        )

    def columns(n):
        if isinstance(n, int):
            return pl.ds(n * cut, cut)
        return pl.ds(pl.multiple_of(n * cut, cut), cut)

    loads = [
        pltpu.make_async_copy(src, dst, load_sem.at[i])
        for i, (src, dst) in enumerate(
            (
                (act_a_hbm, act_a),
                (act_b_hbm, act_b),
                (cot_b_hbm, cot_b),
                (w_gate, own_g),
                (w_up, own_u),
                (w_down, own_d),
            )
        )
    ]
    for load in loads:
        load.start()

    partners = [x_dev, y_dev] + [ahead(step) for step in range(1, experts)] + [next_pipe]
    if n_pipe > 2:
        partners.append(last_pipe)
    barrier = pltpu.get_barrier_semaphore()
    for partner in partners:
        pl.semaphore_signal(barrier, inc=1, device_id=partner, device_id_type=MESH)
    pl.semaphore_wait(barrier, len(partners))

    w_copies = [
        remote(w_gate, oth_g, w_send.at[0], w_recv.at[0], x_dev),
        remote(w_up, oth_u, w_send.at[1], w_recv.at[1], x_dev),
    ]

    def down_copy(n):
        cols = columns(n)
        return remote(
            w_down.at[:, cols], oth_d.at[:, cols], w_send.at[2 + n], w_recv.at[2 + n], x_dev
        )

    for copy in w_copies:
        copy.start()
    for n in range(CHUNKS):
        down_copy(n).start()

    def z_copy(i, send, into, step):
        return remote(
            send.at[step], into.at[0, step], z_send.at[i, step], z_recv.at[i, step], ahead(step)
        )

    def y_copy(i, into, step):
        return remote(
            into.at[0, step], into.at[1, step], y_send.at[i, step], y_recv.at[i, step], y_dev
        )

    def block_of(index):
        count = jnp.zeros_like(index)
        for step in range(1, experts):
            count = count + jnp.where(index >= step * slot, 1, 0)
        place = (index - count * slot).astype(jnp.float32)
        expert = count + mine
        return jnp.where(expert >= experts, expert - experts, expert), place

    def ids_columns(idst):
        first = lax.broadcasted_iota(jnp.int32, (tokens, tokens), 0)
        second = lax.broadcasted_iota(jnp.int32, (tokens, tokens), 1)
        return [
            jnp.sum(
                jnp.where(first == second, idst[k : k + 1, :].astype(jnp.float32), 0.0),
                axis=1,
                keepdims=True,
            )
            for k in range(top)
        ]

    gain_row = gain[...].astype(jnp.float32)

    def normalize(act):
        values = act[...].astype(jnp.float32)
        inverse = lax.rsqrt(jnp.mean(values * values, axis=-1, keepdims=True) + norm_eps)
        normed[...] = (values * inverse * gain_row).astype(jnp.bfloat16)
        return inverse

    def route(ids):
        logits = dot_last(normed[...], router[...])
        number = lax.broadcasted_iota(jnp.int32, logits.shape, 1).astype(jnp.float32)
        scores = [
            jax.nn.sigmoid(
                jnp.sum(
                    jnp.where(ids[k] == number, logits, 0.0), axis=1, keepdims=True
                )
            )
            for k in range(top)
        ]
        whole = functools.reduce(lambda a, b: a + b, scores)
        return scores, [score / whole for score in scores], whole

    def pack_mask(idst):
        expert, place = block_of(lax.broadcasted_iota(jnp.int32, (total_slots, tokens), 0))
        named = jnp.zeros((total_slots, tokens), jnp.float32)
        for k in range(top):
            named = named + jnp.where(idst[k : k + 1, :] == expert, 1.0, 0.0)
        first = lax.broadcasted_iota(jnp.int32, (tokens, tokens), 0)
        second = lax.broadcasted_iota(jnp.int32, (tokens, tokens), 1)
        upper = jnp.where(first <= second, 1.0, 0.0).astype(jnp.bfloat16)
        count = dot(named.astype(jnp.bfloat16), upper)
        return jnp.where(count - 1.0 == place, named, 0.0).astype(jnp.bfloat16)

    def unpack_masks(ids):
        expert, place = block_of(lax.broadcasted_iota(jnp.int32, (tokens, total_slots), 1))
        expert = expert.astype(jnp.float32)
        hits = [jnp.where(ids[k] == expert, 1.0, 0.0) for k in range(top)]
        named = functools.reduce(lambda a, b: a + b, hits)
        first = lax.broadcasted_iota(jnp.int32, (tokens, tokens), 0)
        second = lax.broadcasted_iota(jnp.int32, (tokens, tokens), 1)
        lower = jnp.where(second <= first, 1.0, 0.0).astype(jnp.bfloat16)
        count = dot(lower, named.astype(jnp.bfloat16))
        return [jnp.where(count - 1.0 == place, hit, 0.0).astype(jnp.bfloat16) for hit in hits]

    def pack(i, mask, source, send, into):
        def body(n, carry):
            cols = columns(n)
            packed = dot(mask, source[:, cols]).reshape(experts, slot, cut).astype(jnp.bfloat16)
            send[:, :, cols] = packed
            into[0, 0, :, cols] = packed[0]
            return carry

        lax.fori_loop(0, CHUNKS, body, 0)
        for step in range(1, experts):
            z_copy(i, send, into, step).start()
        y_copy(i, into, 0).start()

    def forward_blocks(i, send, into):
        for step in range(1, experts):
            z_copy(i, send, into, step).wait_recv()
            y_copy(i, into, step).start()

    def arrived(i, into):
        for step in range(experts):
            y_copy(i, into, step).wait_recv()

    ids_a = ids_columns(idst_a)
    ids_b = ids_columns(idst_b)
    for load in loads[:3]:
        load.wait()
    inverse_a = normalize(act_a)
    share_a = route(ids_a)[1]
    pack(0, pack_mask(idst_a), normed, send_a, rows_a)
    inverse_b = normalize(act_b)
    mask_b = pack_mask(idst_b)
    pack(1, mask_b, normed, send_b, rows_b)
    pack(2, mask_b, cot_b, send_c, rows_c)
    scores_b, share_b, whole_b = route(ids_b)

    def project(into, gate_w, up_w, half):
        lanes = pl.ds(half * hidden, hidden)

        def body(n, carry):
            cols = columns(n)
            part = into[:, :, :, cols].reshape(rows, cut)
            gate = dot(part, gate_w[cols, :])
            up = dot(part, up_w[cols, :])

            @pl.when(n == 0)
            def _():
                gate_s[:, lanes] = gate
                up_s[:, lanes] = up

            @pl.when(n > 0)
            def _():
                gate_s[:, lanes] += gate
                up_s[:, lanes] += up

            return carry

        lax.fori_loop(0, CHUNKS, body, 0)

    def grad_hidden(n, down_w, half):
        lanes = pl.ds(half * hidden, hidden)
        cols = columns(n)
        part = rows_c[:, :, :, cols].reshape(rows, cut)
        gact_s[:, lanes] += dot_last(part, down_w[:, cols])

    def activate(half):
        lanes = pl.ds(half * hidden, hidden)
        gate = gate_s[:, lanes]
        mid_a[:, lanes] = (gate * jax.nn.sigmoid(gate) * up_s[:, lanes]).astype(jnp.bfloat16)

    def prepare(half):
        lanes = pl.ds(half * hidden, hidden)
        gate = gate_s[:, lanes]
        up = up_s[:, lanes]
        sig = jax.nn.sigmoid(gate)
        swish = gate * sig
        mid_x[:, lanes] = (swish * up).astype(jnp.bfloat16)
        gate_s[:, lanes] = up * sig * (1.0 + gate * (1.0 - sig))
        up_s[:, lanes] = swish

    def finalize(half):
        lanes = pl.ds(half * hidden, hidden)
        gact = gact_s[:, lanes]
        mid_g[:, lanes] = (gact * gate_s[:, lanes]).astype(jnp.bfloat16)
        mid_u[:, lanes] = (gact * up_s[:, lanes]).astype(jnp.bfloat16)
        return jnp.sum(mid_x[:, lanes].astype(jnp.float32) * gact, axis=-1, keepdims=True)

    forward_blocks(0, send_a, rows_a)
    for load in loads[3:]:
        load.wait()
    forward_blocks(1, send_b, rows_b)
    arrived(0, rows_a)
    project(rows_a, own_g, own_u, 0)
    activate(0)
    forward_blocks(2, send_c, rows_c)
    for step in range(1, experts):
        z_copy(0, send_a, rows_a, step).wait_send()
        z_copy(1, send_b, rows_b, step).wait_send()
    zsend_a, zsend_b = send_a, send_b
    arrived(1, rows_b)
    project(rows_b, own_g, own_u, 0)
    prepare(0)
    gact_s[...] = jnp.zeros_like(gact_s)
    arrived(2, rows_c)

    def own_grad(n, carry):
        grad_hidden(n, own_d, 0)
        return carry

    lax.fori_loop(0, CHUNKS, own_grad, 0)

    contract_own = finalize(0)

    def own_part(n, carry):
        cols = columns(n)
        part_b[:, cols] = dot_last(mid_g[:, :hidden], own_g[cols, :]) + dot_last(
            mid_u[:, :hidden], own_u[cols, :]
        )
        return carry

    lax.fori_loop(0, CHUNKS, own_part, 0)

    for copy in w_copies:
        copy.wait_recv()
    project(rows_a, oth_g, oth_u, 1)
    activate(1)
    project(rows_b, oth_g, oth_u, 1)
    prepare(1)

    def yb_copy(i, n, source, into):
        cols = columns(n)
        return remote(
            source.at[:, :, cols], into.at[:, :, cols], yb_send.at[i, n], yb_recv.at[i, n], y_dev
        )

    def zb_copy(i, n, source, into, step):
        cols = columns(n)
        return remote(
            source.at[step, :, cols],
            into.at[step, :, cols],
            zb_send.at[i, n, step],
            zb_recv.at[i, n, step],
            behind(step),
        )

    def split_out(i, n, out, near, source, into):
        cols = columns(n)
        near[:total_slots, cols] = out[:total_slots]
        far = out[total_slots:].reshape(experts, slot, cut)
        source[:, :, cols] = far.astype(jnp.bfloat16)
        yb_copy(i, n, source, into).start()

    def join(i, n, near, ysource, yinto, zsource, zinto):
        cols = columns(n)
        yb_copy(i, n, ysource, yinto).wait_recv()
        kept = near[:total_slots, cols].reshape(experts, slot, cut)
        summed = kept + yinto[:, :, cols].astype(jnp.float32)
        summed = summed.astype(jnp.bfloat16)
        zsource[:, :, cols] = summed
        zinto[0, :, cols] = summed[0]
        for step in range(1, experts):
            zb_copy(i, n, zsource, zinto, step).start()

    def down_step(n):
        cols = columns(n)
        down_copy(n).wait_recv()
        out = dot(mid_a[:, :hidden], own_d[:, cols]) + dot(mid_a[:, hidden:], oth_d[:, cols])
        split_out(0, n, out, near_a, ysend_a, yback_a)
        grad_hidden(n, oth_d, 1)

    def join_a(n):
        join(0, n, near_a, ysend_a, yback_a, zsend_a, home_a)

    def down_loop(n, carry):
        down_step(n)
        join_a(n - 1)
        return carry

    down_step(0)
    lax.fori_loop(1, CHUNKS - 1, down_loop, 0)
    down_step(CHUNKS - 1)
    contract = jnp.broadcast_to(
        contract_own + finalize(1), (rows, LANES)
    )
    ysend_c[...] = contract[total_slots:].reshape(experts, slot, LANES).astype(jnp.bfloat16)
    near_c = contract[:total_slots].reshape(experts, slot, LANES)
    yc_copy = remote(ysend_c, yback_c, yb_send.at[1, CHUNKS], yb_recv.at[1, CHUNKS], y_dev)

    def zc_copy(step):
        return remote(
            zsend_c.at[step],
            home_c.at[step],
            zb_send.at[1, CHUNKS, step],
            zb_recv.at[1, CHUNKS, step],
            behind(step),
        )

    def grad_step(n):
        cols = columns(n)
        out = dot_last(mid_g[:, hidden:], oth_g[cols, :])
        out = out + dot_last(mid_u[:, hidden:], oth_u[cols, :])
        out = out + part_b[:, cols]
        split_out(1, n, out, part_b, ysend_b, yback_b)

    def join_b(n):
        join(1, n, part_b, ysend_b, yback_b, zsend_b, home_b)

    grad_step(0)
    yc_copy.start()
    join_a(CHUNKS - 2)
    grad_step(1)
    join_a(CHUNKS - 1)
    join_b(0)
    yc_copy.wait_recv()
    summed_c = (near_c + yback_c[...].astype(jnp.float32)).astype(jnp.bfloat16)
    zsend_c[...] = summed_c
    home_c[0] = summed_c[0]
    for step in range(1, experts):
        zc_copy(step).start()

    def grad_loop(n, carry):
        grad_step(n)
        join_b(n - 1)
        return carry

    lax.fori_loop(2, CHUNKS, grad_loop, 0)
    join_b(CHUNKS - 1)

    def mix(i, n, zsource, zinto, masks, share):
        cols = columns(n)
        for step in range(1, experts):
            zb_copy(i, n, zsource, zinto, step).wait_recv()
        block = zinto[:, :, cols].reshape(total_slots, cut)
        return functools.reduce(
            lambda a, b: a + b, [share[k] * dot(masks[k], block) for k in range(top)]
        )

    masks_a = unpack_masks(ids_a)

    def finish_a(n, carry):
        cols = columns(n)
        mixed = mix(0, n, zsend_a, home_a, masks_a, share_a)
        values = act_a[:, cols].astype(jnp.float32)
        sect_a[:, cols] = (values + route_scale * mixed).astype(jnp.bfloat16)
        return carry

    lax.fori_loop(0, CHUNKS, finish_a, 0)
    pa_copy = remote(sect_a, next_a, p_send.at[0], p_recv.at[0], next_pipe)
    pa_copy.start()

    masks_b = unpack_masks(ids_b)
    for step in range(1, experts):
        zc_copy(step).wait_recv()
    home = home_c[...].reshape(total_slots, LANES)
    grad_share = [route_scale * dot(masks_b[k], home)[:, :1] for k in range(top)]
    center = functools.reduce(
        lambda a, b: a + b, [share_b[k] * grad_share[k] for k in range(top)]
    )
    number = lax.broadcasted_iota(jnp.int32, (tokens, router.shape[0]), 1).astype(jnp.float32)
    dense = jnp.zeros((tokens, router.shape[0]), jnp.float32)
    for k in range(top):
        grad_score = (grad_share[k] - center) / whole_b
        grad_logit = grad_score * scores_b[k] * (1.0 - scores_b[k])
        dense = dense + jnp.where(ids_b[k] == number, grad_logit, 0.0)
    dense = dense.astype(jnp.bfloat16)

    def finish_b(n, inner):
        cols = columns(n)
        branch = mix(1, n, zsend_b, home_b, masks_b, share_b)
        term = dot(dense, router[:, cols])
        grad = (route_scale * branch + term) * gain[:, cols].astype(jnp.float32)
        grad_n[:, cols] = grad
        values = act_b[:, cols].astype(jnp.float32)
        return inner + jnp.sum(values * grad, axis=-1, keepdims=True)

    inner = lax.fori_loop(0, CHUNKS, finish_b, jnp.zeros((tokens, 1), jnp.float32))
    scale = inverse_b * inverse_b * inverse_b * (inner / width)

    def write_b(n, carry):
        cols = columns(n)
        values = act_b[:, cols].astype(jnp.float32)
        out = cot_b[:, cols].astype(jnp.float32) + inverse_b * grad_n[:, cols] - values * scale
        sect_b[:, cols] = out.astype(jnp.bfloat16)
        return carry

    lax.fori_loop(0, CHUNKS, write_b, 0)
    pb_copy = remote(sect_b, next_b, p_send.at[1], p_recv.at[1], last_pipe)
    pb_copy.start()

    for copy in w_copies:
        copy.wait_send()
    for i, (send, into) in enumerate(((send_a, rows_a), (send_b, rows_b), (send_c, rows_c))):
        y_copy(i, into, 0).wait_send()
        for step in range(1, experts):
            if i == 2:
                z_copy(i, send, into, step).wait_send()
            y_copy(i, into, step).wait_send()

    def drain(n, carry):
        down_copy(n).wait_send()
        yb_copy(0, n, ysend_a, yback_a).wait_send()
        yb_copy(1, n, ysend_b, yback_b).wait_send()
        for step in range(1, experts):
            zb_copy(0, n, zsend_a, home_a, step).wait_send()
            zb_copy(1, n, zsend_b, home_b, step).wait_send()
        return carry

    lax.fori_loop(0, CHUNKS, drain, 0)
    yc_copy.wait_send()
    for step in range(1, experts):
        zc_copy(step).wait_send()
    pa_copy.wait()
    pb_copy.wait()


def hand_out(from_a, from_b, into_a, into_b, sems):
    share = from_a.shape[0] // HAND_PARTS
    copies = []
    for i, (src, dst) in enumerate(((from_a, into_a), (from_b, into_b))):
        for part in range(HAND_PARTS):
            lines = pl.ds(part * share, share)
            copies.append(pltpu.make_async_copy(src.at[lines], dst.at[lines], sems.at[i, part]))
    for copy in copies:
        copy.start()
    for copy in copies:
        copy.wait()


def per_device(act_a, ids_a, act_b, cot_b, ids_b, norm_gain, router, w_gate, w_up, w_down):
    n_expert = lax.axis_size("expert")
    n_pipe = lax.axis_size("pipe")
    experts = n_expert // SPLIT
    tokens, width = act_a.shape[1:]
    top = ids_a.shape[2]
    hidden = w_gate.shape[3]
    capacity = min(tokens, max(2, 5 * tokens * top // (4 * experts)))
    slot = -(-capacity // SLOT_ROWS) * SLOT_ROWS
    slots = experts * slot
    rows = 2 * slots
    sizes = (n_expert, n_pipe, experts, slot, top, width, hidden, tokens)

    def half(*dims):
        return pltpu.VMEM(dims, jnp.bfloat16)

    def full(*dims):
        return pltpu.VMEM(dims, jnp.float32)

    sem = pltpu.SemaphoreType.DMA
    block = (experts, slot, width)
    narrow = (experts, slot, LANES)
    vmem = pl.BlockSpec(memory_space=pltpu.VMEM)
    anywhere = pl.BlockSpec(memory_space=pl.ANY)
    out = jax.ShapeDtypeStruct((tokens, width), jnp.bfloat16)
    next_a, next_b = pl.pallas_call(
        functools.partial(kernel, sizes),
        out_shape=(out, out),
        in_specs=[anywhere] * 3 + [vmem] * 4 + [anywhere] * 3,
        out_specs=(anywhere, anywhere),
        scratch_shapes=[
            half(width, hidden),
            half(width, hidden),
            half(hidden, width),
            half(width, hidden),
            half(width, hidden),
            half(hidden, width),
            half(tokens, width),
            half(tokens, width),
            half(tokens, width),
            half(tokens, width),
            half(*block),
            half(*block),
            half(*block),
            half(2, *block),
            half(2, *block),
            half(2, *block),
            full(rows, 2 * hidden),
            full(rows, 2 * hidden),
            full(rows, 2 * hidden),
            half(rows, 2 * hidden),
            half(rows, 2 * hidden),
            half(rows, 2 * hidden),
            half(rows, 2 * hidden),
            full(slots, width),
            full(rows, width),
            half(*block),
            half(*block),
            half(*narrow),
            half(*block),
            half(*block),
            half(*narrow),
            half(*narrow),
            half(*block),
            half(*block),
            half(*narrow),
            full(tokens, width),
            half(tokens, width),
            half(tokens, width),
            sem((6,)),
            sem((2 + CHUNKS,)),
            sem((2 + CHUNKS,)),
            sem((3, experts)),
            sem((3, experts)),
            sem((3, experts)),
            sem((3, experts)),
            sem((2, CHUNKS + 1)),
            sem((2, CHUNKS + 1)),
            sem((2, CHUNKS + 1, experts)),
            sem((2, CHUNKS + 1, experts)),
            sem((2,)),
            sem((2,)),
        ],
        compiler_params=pltpu.CompilerParams(
            collective_id=0, has_side_effects=True, vmem_limit_bytes=60 * 1024 * 1024
        ),
        cost_estimate=pl.CostEstimate(
            flops=2 * 9 * rows * width * hidden * 2,
            bytes_accessed=6 * width * hidden * 2,
            transcendentals=0,
        ),
    )(
        act_a[0],
        act_b[0],
        cot_b[0],
        ids_a[0].T,
        ids_b[0].T,
        norm_gain,
        router[0].T,
        w_gate[0, 0],
        w_up[0, 0],
        w_down[0, 0],
    )
    next_a, next_b = pl.pallas_call(
        hand_out,
        out_shape=(out, out),
        in_specs=[anywhere] * 2,
        out_specs=(anywhere, anywhere),
        scratch_shapes=[sem((2, HAND_PARTS))],
    )(next_a, next_b)
    return (next_a[None], next_b[None])


SLOT_ROWS = 8
HAND_PARTS = 4


def solution(mesh):
    return jax.shard_map(
        per_device,
        mesh=mesh,
        in_specs=(
            P("pipe", "expert", None),
            P("pipe", "expert", None),
            P("pipe", "expert", None),
            P("pipe", "expert", None),
            P("pipe", "expert", None),
            P("pipe", None),
            P("pipe", None, None),
            P("pipe", "expert", None, None),
            P("pipe", "expert", None, None),
            P("pipe", "expert", None, None),
        ),
        out_specs=(P("pipe", "expert", None), P("pipe", "expert", None)),
        check_vma=False,
    )
```

```python
import functools
import jax
import jax.numpy as jnp
from jax import lax
from jax.experimental import pallas as pl
from jax.experimental.pallas import tpu as pltpu
from jax.sharding import PartitionSpec as P

SPLIT = 4
CHUNKS = 7
LANES = 128
MESH = pl.DeviceIdType.MESH

route_scale = 2.5
norm_eps = 1e-06
last_dims = (((1,), (1,)), ((), ()))


def dot(left, right):
    return jnp.dot(left, right, preferred_element_type=jnp.float32)


def dot_last(left, right):
    return lax.dot_general(left, right, last_dims, preferred_element_type=jnp.float32)


def kernel(
    sizes,
    act_a_hbm,
    act_b_hbm,
    cot_b_hbm,
    idst_a,
    idst_b,
    gain,
    router,
    w_gate,
    w_up,
    w_down,
    next_a,
    next_b,
    own_g,
    own_u,
    own_d,
    oth_g,
    oth_u,
    oth_d,
    act_a,
    act_b,
    cot_b,
    normed,
    send_a,
    send_b,
    send_c,
    rows_a,
    rows_b,
    rows_c,
    gate_s,
    up_s,
    gact_s,
    mid_a,
    mid_g,
    mid_u,
    mid_x,
    near_a,
    part_b,
    ysend_a,
    ysend_b,
    ysend_c,
    yback_a,
    yback_b,
    yback_c,
    zsend_c,
    home_a,
    home_b,
    home_c,
    grad_n,
    sect_a,
    sect_b,
    load_sem,
    w_send,
    w_recv,
    z_send,
    z_recv,
    y_send,
    y_recv,
    yb_send,
    yb_recv,
    zb_send,
    zb_recv,
    p_send,
    p_recv,
):
    n_expert, n_pipe, experts, slot, top, width, hidden, tokens = sizes
    total_slots = experts * slot
    rows = 2 * total_slots
    cut = width // CHUNKS
    me = lax.axis_index("expert")
    pipe = lax.axis_index("pipe")
    mine = me // SPLIT
    x_dev = {"expert": me + 1 - 2 * (me % 2)}
    y_dev = {"expert": me + 2 - 4 * ((me // 2) % 2)}

    def ahead(step):
        return {"expert": (me + SPLIT * step) % n_expert}

    def behind(step):
        return {"expert": (me + n_expert - SPLIT * step) % n_expert}

    next_pipe = {"pipe": (pipe + 1) % n_pipe}
    last_pipe = {"pipe": (pipe + n_pipe - 1) % n_pipe}

    def remote(src, dst, send, recv, device):
        return pltpu.make_async_remote_copy(
            src_ref=src,
            dst_ref=dst,
            send_sem=send,
            recv_sem=recv,
            device_id=device,
            device_id_type=MESH,
        )

    def columns(n):
        if isinstance(n, int):
            return pl.ds(n * cut, cut)
        return pl.ds(pl.multiple_of(n * cut, cut), cut)

    loads = [
        pltpu.make_async_copy(src, dst, load_sem.at[i])
        for i, (src, dst) in enumerate(
            (
                (act_a_hbm, act_a),
                (act_b_hbm, act_b),
                (cot_b_hbm, cot_b),
                (w_gate, own_g),
                (w_up, own_u),
                (w_down, own_d),
            )
        )
    ]
    for load in loads:
        load.start()

    partners = [x_dev, y_dev] + [ahead(step) for step in range(1, experts)] + [next_pipe]
    if n_pipe > 2:
        partners.append(last_pipe)
    barrier = pltpu.get_barrier_semaphore()
    for partner in partners:
        pl.semaphore_signal(barrier, inc=1, device_id=partner, device_id_type=MESH)
    pl.semaphore_wait(barrier, len(partners))

    w_copies = [
        remote(w_gate, oth_g, w_send.at[0], w_recv.at[0], x_dev),
        remote(w_up, oth_u, w_send.at[1], w_recv.at[1], x_dev),
    ]

    def down_copy(n):
        cols = columns(n)
        return remote(
            w_down.at[:, cols], oth_d.at[:, cols], w_send.at[2 + n], w_recv.at[2 + n], x_dev
        )

    for copy in w_copies:
        copy.start()

    def z_copy(i, send, into, step):
        return remote(
            send.at[step], into.at[0, step], z_send.at[i, step], z_recv.at[i, step], ahead(step)
        )

    def y_copy(i, into, step):
        return remote(
            into.at[0, step], into.at[1, step], y_send.at[i, step], y_recv.at[i, step], y_dev
        )

    def block_of(index):
        count = jnp.zeros_like(index)
        for step in range(1, experts):
            count = count + jnp.where(index >= step * slot, 1, 0)
        place = (index - count * slot).astype(jnp.float32)
        expert = count + mine
        return jnp.where(expert >= experts, expert - experts, expert), place

    def ids_columns(idst):
        first = lax.broadcasted_iota(jnp.int32, (tokens, tokens), 0)
        second = lax.broadcasted_iota(jnp.int32, (tokens, tokens), 1)
        return [
            jnp.sum(
                jnp.where(first == second, idst[k : k + 1, :].astype(jnp.float32), 0.0),
                axis=1,
                keepdims=True,
            )
            for k in range(top)
        ]

    gain_row = gain[...].astype(jnp.float32)

    def normalize(act):
        values = act[...].astype(jnp.float32)
        inverse = lax.rsqrt(jnp.mean(values * values, axis=-1, keepdims=True) + norm_eps)
        normed[...] = (values * inverse * gain_row).astype(jnp.bfloat16)
        return inverse

    def route(ids):
        logits = dot_last(normed[...], router[...])
        number = lax.broadcasted_iota(jnp.int32, logits.shape, 1).astype(jnp.float32)
        scores = [
            jax.nn.sigmoid(
                jnp.sum(
                    jnp.where(ids[k] == number, logits, 0.0), axis=1, keepdims=True
                )
            )
            for k in range(top)
        ]
        whole = functools.reduce(lambda a, b: a + b, scores)
        return scores, [score / whole for score in scores], whole

    def pack_mask(idst):
        expert, place = block_of(lax.broadcasted_iota(jnp.int32, (total_slots, tokens), 0))
        named = jnp.zeros((total_slots, tokens), jnp.float32)
        for k in range(top):
            named = named + jnp.where(idst[k : k + 1, :] == expert, 1.0, 0.0)
        first = lax.broadcasted_iota(jnp.int32, (tokens, tokens), 0)
        second = lax.broadcasted_iota(jnp.int32, (tokens, tokens), 1)
        upper = jnp.where(first <= second, 1.0, 0.0).astype(jnp.bfloat16)
        count = dot(named.astype(jnp.bfloat16), upper)
        return jnp.where(count - 1.0 == place, named, 0.0).astype(jnp.bfloat16)

    def unpack_masks(ids):
        expert, place = block_of(lax.broadcasted_iota(jnp.int32, (tokens, total_slots), 1))
        expert = expert.astype(jnp.float32)
        hits = [jnp.where(ids[k] == expert, 1.0, 0.0) for k in range(top)]
        named = functools.reduce(lambda a, b: a + b, hits)
        first = lax.broadcasted_iota(jnp.int32, (tokens, tokens), 0)
        second = lax.broadcasted_iota(jnp.int32, (tokens, tokens), 1)
        lower = jnp.where(second <= first, 1.0, 0.0).astype(jnp.bfloat16)
        count = dot(lower, named.astype(jnp.bfloat16))
        return [jnp.where(count - 1.0 == place, hit, 0.0).astype(jnp.bfloat16) for hit in hits]

    def pack(i, mask, source, send, into):
        def body(n, carry):
            cols = columns(n)
            packed = dot(mask, source[:, cols]).reshape(experts, slot, cut).astype(jnp.bfloat16)
            send[:, :, cols] = packed
            into[0, 0, :, cols] = packed[0]
            return carry

        lax.fori_loop(0, CHUNKS, body, 0)

    def forward_blocks(i, send, into, follow=None):
        for step in range(1, experts):
            z_copy(i, send, into, step).wait_recv()
            y_copy(i, into, step).start()
            z_copy(i, send, into, step).wait_send()
            if follow is not None:
                z_copy(i + 1, *follow, step).start()
        if follow is not None:
            y_copy(i + 1, follow[1], 0).start()

    def arrived(i, into):
        for step in range(experts):
            y_copy(i, into, step).wait_recv()

    ids_a = ids_columns(idst_a)
    ids_b = ids_columns(idst_b)
    for load in loads[:3]:
        load.wait()
    inverse_a = normalize(act_a)
    share_a = route(ids_a)[1]
    pack(0, pack_mask(idst_a), normed, send_a, rows_a)
    for step in range(1, experts):
        z_copy(0, send_a, rows_a, step).start()
    y_copy(0, rows_a, 0).start()
    inverse_b = normalize(act_b)
    mask_b = pack_mask(idst_b)
    pack(1, mask_b, normed, send_b, rows_b)
    pack(2, mask_b, cot_b, send_c, rows_c)
    scores_b, share_b, whole_b = route(ids_b)

    def project(into, gate_w, up_w, half):
        lanes = pl.ds(half * hidden, hidden)

        def body(n, carry):
            cols = columns(n)
            part = into[:, :, :, cols].reshape(rows, cut)
            gate = dot(part, gate_w[cols, :])
            up = dot(part, up_w[cols, :])

            @pl.when(n == 0)
            def _():
                gate_s[:, lanes] = gate
                up_s[:, lanes] = up

            @pl.when(n > 0)
            def _():
                gate_s[:, lanes] += gate
                up_s[:, lanes] += up

            return carry

        lax.fori_loop(0, CHUNKS, body, 0)

    def grad_hidden(n, down_w, half):
        lanes = pl.ds(half * hidden, hidden)
        cols = columns(n)
        part = rows_c[:, :, :, cols].reshape(rows, cut)
        gact_s[:, lanes] += dot_last(part, down_w[:, cols])

    def activate(half):
        lanes = pl.ds(half * hidden, hidden)
        gate = gate_s[:, lanes]
        mid_a[:, lanes] = (gate * jax.nn.sigmoid(gate) * up_s[:, lanes]).astype(jnp.bfloat16)

    def prepare(half):
        lanes = pl.ds(half * hidden, hidden)
        gate = gate_s[:, lanes]
        up = up_s[:, lanes]
        sig = jax.nn.sigmoid(gate)
        swish = gate * sig
        mid_x[:, lanes] = (swish * up).astype(jnp.bfloat16)
        gate_s[:, lanes] = up * sig * (1.0 + gate * (1.0 - sig))
        up_s[:, lanes] = swish

    def finalize(half):
        lanes = pl.ds(half * hidden, hidden)
        gact = gact_s[:, lanes]
        mid_g[:, lanes] = (gact * gate_s[:, lanes]).astype(jnp.bfloat16)
        mid_u[:, lanes] = (gact * up_s[:, lanes]).astype(jnp.bfloat16)
        return jnp.sum(mid_x[:, lanes].astype(jnp.float32) * gact, axis=-1, keepdims=True)

    forward_blocks(0, send_a, rows_a, (send_b, rows_b))
    for load in loads[3:]:
        load.wait()
    arrived(0, rows_a)
    project(rows_a, own_g, own_u, 0)
    activate(0)
    forward_blocks(1, send_b, rows_b, (send_c, rows_c))
    zsend_a, zsend_b = send_a, send_b
    down_copy(0).start()
    arrived(1, rows_b)
    project(rows_b, own_g, own_u, 0)
    prepare(0)
    forward_blocks(2, send_c, rows_c)
    down_copy(1).start()
    gact_s[...] = jnp.zeros_like(gact_s)
    arrived(2, rows_c)

    def own_grad(n, carry):
        grad_hidden(n, own_d, 0)
        return carry

    lax.fori_loop(0, CHUNKS, own_grad, 0)

    contract_own = finalize(0)

    def own_part(n, carry):
        cols = columns(n)
        part_b[:, cols] = dot_last(mid_g[:, :hidden], own_g[cols, :]) + dot_last(
            mid_u[:, :hidden], own_u[cols, :]
        )
        return carry

    lax.fori_loop(0, CHUNKS, own_part, 0)

    for copy in w_copies:
        copy.wait_recv()
    project(rows_a, oth_g, oth_u, 1)
    activate(1)
    project(rows_b, oth_g, oth_u, 1)
    prepare(1)

    def yb_copy(i, n, source, into):
        cols = columns(n)
        return remote(
            source.at[:, :, cols], into.at[:, :, cols], yb_send.at[i, n], yb_recv.at[i, n], y_dev
        )

    def zb_copy(i, n, source, into, step):
        cols = columns(n)
        return remote(
            source.at[step, :, cols],
            into.at[step, :, cols],
            zb_send.at[i, n, step],
            zb_recv.at[i, n, step],
            behind(step),
        )

    def split_out(i, n, out, near, source, into):
        cols = columns(n)
        near[:total_slots, cols] = out[:total_slots]
        far = out[total_slots:].reshape(experts, slot, cut)
        source[:, :, cols] = far.astype(jnp.bfloat16)
        yb_copy(i, n, source, into).start()

    def join(i, n, near, ysource, yinto, zsource, zinto):
        cols = columns(n)
        yb_copy(i, n, ysource, yinto).wait_recv()
        kept = near[:total_slots, cols].reshape(experts, slot, cut)
        summed = kept + yinto[:, :, cols].astype(jnp.float32)
        summed = summed.astype(jnp.bfloat16)
        zsource[:, :, cols] = summed
        zinto[0, :, cols] = summed[0]
        for step in range(1, experts):
            zb_copy(i, n, zsource, zinto, step).start()

    def down_step(n):
        cols = columns(n)
        down_copy(n).wait_recv()
        if isinstance(n, int):
            if n + 2 < CHUNKS:
                down_copy(n + 2).start()
        else:

            @pl.when(n + 2 < CHUNKS)
            def _():
                down_copy(n + 2).start()

        out = dot(mid_a[:, :hidden], own_d[:, cols]) + dot(mid_a[:, hidden:], oth_d[:, cols])
        split_out(0, n, out, near_a, ysend_a, yback_a)
        grad_hidden(n, oth_d, 1)

    def join_a(n):
        join(0, n, near_a, ysend_a, yback_a, zsend_a, home_a)

    def down_loop(n, carry):
        down_step(n)
        join_a(n - 1)
        return carry

    down_step(0)
    lax.fori_loop(1, CHUNKS - 1, down_loop, 0)
    down_step(CHUNKS - 1)
    contract = jnp.broadcast_to(
        contract_own + finalize(1), (rows, LANES)
    )
    ysend_c[...] = contract[total_slots:].reshape(experts, slot, LANES).astype(jnp.bfloat16)
    near_c = contract[:total_slots].reshape(experts, slot, LANES)
    yc_copy = remote(ysend_c, yback_c, yb_send.at[1, CHUNKS], yb_recv.at[1, CHUNKS], y_dev)

    def zc_copy(step):
        return remote(
            zsend_c.at[step],
            home_c.at[step],
            zb_send.at[1, CHUNKS, step],
            zb_recv.at[1, CHUNKS, step],
            behind(step),
        )

    def grad_step(n):
        cols = columns(n)
        out = dot_last(mid_g[:, hidden:], oth_g[cols, :])
        out = out + dot_last(mid_u[:, hidden:], oth_u[cols, :])
        out = out + part_b[:, cols]
        split_out(1, n, out, part_b, ysend_b, yback_b)

    def join_b(n):
        join(1, n, part_b, ysend_b, yback_b, zsend_b, home_b)

    grad_step(0)
    yc_copy.start()
    join_a(CHUNKS - 2)
    grad_step(1)
    join_a(CHUNKS - 1)
    join_b(0)
    yc_copy.wait_recv()
    summed_c = (near_c + yback_c[...].astype(jnp.float32)).astype(jnp.bfloat16)
    zsend_c[...] = summed_c
    home_c[0] = summed_c[0]
    for step in range(1, experts):
        zc_copy(step).start()

    def grad_loop(n, carry):
        grad_step(n)
        join_b(n - 1)
        return carry

    lax.fori_loop(2, CHUNKS, grad_loop, 0)
    join_b(CHUNKS - 1)

    def mix(i, n, zsource, zinto, masks, share):
        cols = columns(n)
        for step in range(1, experts):
            zb_copy(i, n, zsource, zinto, step).wait_recv()
        block = zinto[:, :, cols].reshape(total_slots, cut)
        return functools.reduce(
            lambda a, b: a + b, [share[k] * dot(masks[k], block) for k in range(top)]
        )

    masks_a = unpack_masks(ids_a)

    def finish_a(n, carry):
        cols = columns(n)
        mixed = mix(0, n, zsend_a, home_a, masks_a, share_a)
        values = act_a[:, cols].astype(jnp.float32)
        sect_a[:, cols] = (values + route_scale * mixed).astype(jnp.bfloat16)
        return carry

    lax.fori_loop(0, CHUNKS, finish_a, 0)
    pa_copy = remote(sect_a, next_a, p_send.at[0], p_recv.at[0], next_pipe)
    pa_copy.start()

    masks_b = unpack_masks(ids_b)
    for step in range(1, experts):
        zc_copy(step).wait_recv()
    home = home_c[...].reshape(total_slots, LANES)
    grad_share = [route_scale * dot(masks_b[k], home)[:, :1] for k in range(top)]
    center = functools.reduce(
        lambda a, b: a + b, [share_b[k] * grad_share[k] for k in range(top)]
    )
    number = lax.broadcasted_iota(jnp.int32, (tokens, router.shape[0]), 1).astype(jnp.float32)
    dense = jnp.zeros((tokens, router.shape[0]), jnp.float32)
    for k in range(top):
        grad_score = (grad_share[k] - center) / whole_b
        grad_logit = grad_score * scores_b[k] * (1.0 - scores_b[k])
        dense = dense + jnp.where(ids_b[k] == number, grad_logit, 0.0)
    dense = dense.astype(jnp.bfloat16)

    def finish_b(n, inner):
        cols = columns(n)
        branch = mix(1, n, zsend_b, home_b, masks_b, share_b)
        term = dot(dense, router[:, cols])
        grad = (route_scale * branch + term) * gain[:, cols].astype(jnp.float32)
        grad_n[:, cols] = grad
        values = act_b[:, cols].astype(jnp.float32)
        return inner + jnp.sum(values * grad, axis=-1, keepdims=True)

    inner = lax.fori_loop(0, CHUNKS, finish_b, jnp.zeros((tokens, 1), jnp.float32))
    scale = inverse_b * inverse_b * inverse_b * (inner / width)

    def write_b(n, carry):
        cols = columns(n)
        values = act_b[:, cols].astype(jnp.float32)
        out = cot_b[:, cols].astype(jnp.float32) + inverse_b * grad_n[:, cols] - values * scale
        sect_b[:, cols] = out.astype(jnp.bfloat16)
        return carry

    lax.fori_loop(0, CHUNKS, write_b, 0)
    pb_copy = remote(sect_b, next_b, p_send.at[1], p_recv.at[1], last_pipe)
    pb_copy.start()

    for copy in w_copies:
        copy.wait_send()
    for i, into in enumerate((rows_a, rows_b, rows_c)):
        for step in range(experts):
            y_copy(i, into, step).wait_send()

    def drain(n, carry):
        down_copy(n).wait_send()
        yb_copy(0, n, ysend_a, yback_a).wait_send()
        yb_copy(1, n, ysend_b, yback_b).wait_send()
        for step in range(1, experts):
            zb_copy(0, n, zsend_a, home_a, step).wait_send()
            zb_copy(1, n, zsend_b, home_b, step).wait_send()
        return carry

    lax.fori_loop(0, CHUNKS, drain, 0)
    yc_copy.wait_send()
    for step in range(1, experts):
        zc_copy(step).wait_send()
    pa_copy.wait()
    pb_copy.wait()


def hand_out(from_a, from_b, into_a, into_b):
    into_a[...] = from_a[...]
    into_b[...] = from_b[...]


def per_device(act_a, ids_a, act_b, cot_b, ids_b, norm_gain, router, w_gate, w_up, w_down):
    n_expert = lax.axis_size("expert")
    n_pipe = lax.axis_size("pipe")
    experts = n_expert // SPLIT
    tokens, width = act_a.shape[1:]
    top = ids_a.shape[2]
    hidden = w_gate.shape[3]
    capacity = min(tokens, max(2, 5 * tokens * top // (4 * experts)))
    slot = -(-capacity // SLOT_ROWS) * SLOT_ROWS
    slots = experts * slot
    rows = 2 * slots
    sizes = (n_expert, n_pipe, experts, slot, top, width, hidden, tokens)

    def half(*dims):
        return pltpu.VMEM(dims, jnp.bfloat16)

    def full(*dims):
        return pltpu.VMEM(dims, jnp.float32)

    sem = pltpu.SemaphoreType.DMA
    block = (experts, slot, width)
    narrow = (experts, slot, LANES)
    vmem = pl.BlockSpec(memory_space=pltpu.VMEM)
    anywhere = pl.BlockSpec(memory_space=pl.ANY)
    out = jax.ShapeDtypeStruct((tokens, width), jnp.bfloat16)
    next_a, next_b = pl.pallas_call(
        functools.partial(kernel, sizes),
        out_shape=(out, out),
        in_specs=[anywhere] * 3 + [vmem] * 4 + [anywhere] * 3,
        out_specs=(anywhere, anywhere),
        scratch_shapes=[
            half(width, hidden),
            half(width, hidden),
            half(hidden, width),
            half(width, hidden),
            half(width, hidden),
            half(hidden, width),
            half(tokens, width),
            half(tokens, width),
            half(tokens, width),
            half(tokens, width),
            half(*block),
            half(*block),
            half(*block),
            half(2, *block),
            half(2, *block),
            half(2, *block),
            full(rows, 2 * hidden),
            full(rows, 2 * hidden),
            full(rows, 2 * hidden),
            half(rows, 2 * hidden),
            half(rows, 2 * hidden),
            half(rows, 2 * hidden),
            half(rows, 2 * hidden),
            full(slots, width),
            full(rows, width),
            half(*block),
            half(*block),
            half(*narrow),
            half(*block),
            half(*block),
            half(*narrow),
            half(*narrow),
            half(*block),
            half(*block),
            half(*narrow),
            full(tokens, width),
            half(tokens, width),
            half(tokens, width),
            sem((6,)),
            sem((2 + CHUNKS,)),
            sem((2 + CHUNKS,)),
            sem((3, experts)),
            sem((3, experts)),
            sem((3, experts)),
            sem((3, experts)),
            sem((2, CHUNKS + 1)),
            sem((2, CHUNKS + 1)),
            sem((2, CHUNKS + 1, experts)),
            sem((2, CHUNKS + 1, experts)),
            sem((2,)),
            sem((2,)),
        ],
        compiler_params=pltpu.CompilerParams(
            collective_id=0, has_side_effects=True, vmem_limit_bytes=60 * 1024 * 1024
        ),
        cost_estimate=pl.CostEstimate(
            flops=2 * 9 * rows * width * hidden * 2,
            bytes_accessed=6 * width * hidden * 2,
            transcendentals=0,
        ),
    )(
        act_a[0],
        act_b[0],
        cot_b[0],
        ids_a[0].T,
        ids_b[0].T,
        norm_gain,
        router[0].T,
        w_gate[0, 0],
        w_up[0, 0],
        w_down[0, 0],
    )
    next_a, next_b = pl.pallas_call(
        hand_out,
        out_shape=(out, out),
        in_specs=[vmem] * 2,
        out_specs=(vmem, vmem),
    )(next_a, next_b)
    return (next_a[None], next_b[None])


SLOT_ROWS = 8


def solution(mesh):
    return jax.shard_map(
        per_device,
        mesh=mesh,
        in_specs=(
            P("pipe", "expert", None),
            P("pipe", "expert", None),
            P("pipe", "expert", None),
            P("pipe", "expert", None),
            P("pipe", "expert", None),
            P("pipe", None),
            P("pipe", None, None),
            P("pipe", "expert", None, None),
            P("pipe", "expert", None, None),
            P("pipe", "expert", None, None),
        ),
        out_specs=(P("pipe", "expert", None), P("pipe", "expert", None)),
        check_vma=False,
    )
```

```python
import functools
import jax
import jax.numpy as jnp
from jax import lax
from jax.experimental import pallas as pl
from jax.experimental.pallas import tpu as pltpu
from jax.sharding import PartitionSpec as P

SPLIT = 4
CHUNKS = 7
AHEAD = 4
LANES = 128
MESH = pl.DeviceIdType.MESH

route_scale = 2.5
norm_eps = 1e-06
last_dims = (((1,), (1,)), ((), ()))


def dot(left, right):
    return jnp.dot(left, right, preferred_element_type=jnp.float32)


def dot_last(left, right):
    return lax.dot_general(left, right, last_dims, preferred_element_type=jnp.float32)


def kernel(
    sizes,
    act_a_hbm,
    act_b_hbm,
    cot_b_hbm,
    idst_a,
    idst_b,
    gain,
    router,
    w_gate,
    w_up,
    w_down,
    next_a,
    next_b,
    own_g,
    own_u,
    own_d,
    oth_g,
    oth_u,
    oth_d,
    act_a,
    act_b,
    cot_b,
    normed,
    send_a,
    send_b,
    send_c,
    rows_a,
    rows_b,
    rows_c,
    gate_s,
    up_s,
    gact_s,
    mid_a,
    mid_g,
    mid_u,
    mid_x,
    near_a,
    near_b,
    ysend_a,
    ysend_b,
    ysend_c,
    yback_a,
    yback_b,
    yback_c,
    zsend_a,
    zsend_b,
    zsend_c,
    home_a,
    home_b,
    home_c,
    grad_n,
    sect_a,
    sect_b,
    load_sem,
    w_send,
    w_recv,
    z_send,
    z_recv,
    y_send,
    y_recv,
    yb_send,
    yb_recv,
    zb_send,
    zb_recv,
    p_send,
    p_recv,
):
    n_expert, n_pipe, experts, slot, top, width, hidden, tokens = sizes
    total_slots = experts * slot
    rows = 2 * total_slots
    cut = width // CHUNKS
    me = lax.axis_index("expert")
    pipe = lax.axis_index("pipe")
    mine = me // SPLIT
    x_dev = {"expert": me + 1 - 2 * (me % 2)}
    y_dev = {"expert": me + 2 - 4 * ((me // 2) % 2)}

    def ahead(step):
        return {"expert": (me + SPLIT * step) % n_expert}

    def behind(step):
        return {"expert": (me + n_expert - SPLIT * step) % n_expert}

    next_pipe = {"pipe": (pipe + 1) % n_pipe}
    last_pipe = {"pipe": (pipe + n_pipe - 1) % n_pipe}

    def remote(src, dst, send, recv, device):
        return pltpu.make_async_remote_copy(
            src_ref=src,
            dst_ref=dst,
            send_sem=send,
            recv_sem=recv,
            device_id=device,
            device_id_type=MESH,
        )

    def columns(n):
        if isinstance(n, int):
            return pl.ds(n * cut, cut)
        return pl.ds(pl.multiple_of(n * cut, cut), cut)

    loads = [
        pltpu.make_async_copy(src, dst, load_sem.at[i])
        for i, (src, dst) in enumerate(
            (
                (act_a_hbm, act_a),
                (act_b_hbm, act_b),
                (cot_b_hbm, cot_b),
                (w_gate, own_g),
                (w_up, own_u),
                (w_down, own_d),
            )
        )
    ]
    for load in loads:
        load.start()

    partners = [x_dev, y_dev] + [ahead(step) for step in range(1, experts)] + [next_pipe]
    if n_pipe > 2:
        partners.append(last_pipe)
    barrier = pltpu.get_barrier_semaphore()
    for partner in partners:
        pl.semaphore_signal(barrier, inc=1, device_id=partner, device_id_type=MESH)
    pl.semaphore_wait(barrier, len(partners))

    w_copies = [
        remote(w_gate, oth_g, w_send.at[0], w_recv.at[0], x_dev),
        remote(w_up, oth_u, w_send.at[1], w_recv.at[1], x_dev),
    ]

    def down_copy(n):
        cols = columns(n)
        return remote(
            w_down.at[:, cols], oth_d.at[:, cols], w_send.at[2 + n], w_recv.at[2 + n], x_dev
        )

    for copy in w_copies:
        copy.start()

    def z_copy(i, send, into, step):
        return remote(
            send.at[step], into.at[0, step], z_send.at[i, step], z_recv.at[i, step], ahead(step)
        )

    def y_copy(i, into, step):
        return remote(
            into.at[0, step], into.at[1, step], y_send.at[i, step], y_recv.at[i, step], y_dev
        )

    def block_of(index):
        count = jnp.zeros_like(index)
        for step in range(1, experts):
            count = count + jnp.where(index >= step * slot, 1, 0)
        place = (index - count * slot).astype(jnp.float32)
        expert = count + mine
        return jnp.where(expert >= experts, expert - experts, expert), place

    def ids_columns(idst):
        first = lax.broadcasted_iota(jnp.int32, (tokens, tokens), 0)
        second = lax.broadcasted_iota(jnp.int32, (tokens, tokens), 1)
        return [
            jnp.sum(
                jnp.where(first == second, idst[k : k + 1, :].astype(jnp.float32), 0.0),
                axis=1,
                keepdims=True,
            )
            for k in range(top)
        ]

    gain_row = gain[...].astype(jnp.float32)

    def normalize(act):
        values = act[...].astype(jnp.float32)
        inverse = lax.rsqrt(jnp.mean(values * values, axis=-1, keepdims=True) + norm_eps)
        normed[...] = (values * inverse * gain_row).astype(jnp.bfloat16)
        return inverse

    def route(ids):
        logits = dot_last(normed[...], router[...])
        number = lax.broadcasted_iota(jnp.int32, logits.shape, 1).astype(jnp.float32)
        scores = [
            jax.nn.sigmoid(
                jnp.sum(
                    jnp.where(ids[k] == number, logits, 0.0), axis=1, keepdims=True
                )
            )
            for k in range(top)
        ]
        whole = functools.reduce(lambda a, b: a + b, scores)
        return scores, [score / whole for score in scores], whole

    def pack_mask(idst):
        expert, place = block_of(lax.broadcasted_iota(jnp.int32, (total_slots, tokens), 0))
        named = jnp.zeros((total_slots, tokens), jnp.float32)
        for k in range(top):
            named = named + jnp.where(idst[k : k + 1, :] == expert, 1.0, 0.0)
        first = lax.broadcasted_iota(jnp.int32, (tokens, tokens), 0)
        second = lax.broadcasted_iota(jnp.int32, (tokens, tokens), 1)
        upper = jnp.where(first <= second, 1.0, 0.0).astype(jnp.bfloat16)
        count = dot(named.astype(jnp.bfloat16), upper)
        return jnp.where(count - 1.0 == place, named, 0.0).astype(jnp.bfloat16)

    def unpack_masks(ids):
        expert, place = block_of(lax.broadcasted_iota(jnp.int32, (tokens, total_slots), 1))
        expert = expert.astype(jnp.float32)
        hits = [jnp.where(ids[k] == expert, 1.0, 0.0) for k in range(top)]
        named = functools.reduce(lambda a, b: a + b, hits)
        first = lax.broadcasted_iota(jnp.int32, (tokens, tokens), 0)
        second = lax.broadcasted_iota(jnp.int32, (tokens, tokens), 1)
        lower = jnp.where(second <= first, 1.0, 0.0).astype(jnp.bfloat16)
        count = dot(lower, named.astype(jnp.bfloat16))
        return [jnp.where(count - 1.0 == place, hit, 0.0).astype(jnp.bfloat16) for hit in hits]

    def pack(i, mask, source, send, into):
        def body(n, carry):
            cols = columns(n)
            packed = dot(mask, source[:, cols]).reshape(experts, slot, cut).astype(jnp.bfloat16)
            send[:, :, cols] = packed
            into[0, 0, :, cols] = packed[0]
            return carry

        lax.fori_loop(0, CHUNKS, body, 0)

    arrays = ((send_a, rows_a), (send_b, rows_b), (send_c, rows_c))
    order = [(i, step) for i in range(3) for step in range(1, experts)]

    def start_z(place):
        if place < len(order):
            i, step = order[place]
            z_copy(i, *arrays[i], step).start()

    def forward_blocks(i):
        for step in range(1, experts):
            z_copy(i, *arrays[i], step).wait_recv()
            y_copy(i, arrays[i][1], step).start()
            z_copy(i, *arrays[i], step).wait_send()
            start_z(order.index((i, step)) + experts)
        if i < 2:
            y_copy(i + 1, arrays[i + 1][1], 0).start()

    def arrived(i, into):
        for step in range(experts):
            y_copy(i, into, step).wait_recv()

    ids_a = ids_columns(idst_a)
    ids_b = ids_columns(idst_b)
    for load in loads[:3]:
        load.wait()
    inverse_a = normalize(act_a)
    share_a = route(ids_a)[1]
    pack(0, pack_mask(idst_a), normed, send_a, rows_a)
    for place in range(experts - 1):
        start_z(place)
    y_copy(0, rows_a, 0).start()
    inverse_b = normalize(act_b)
    mask_b = pack_mask(idst_b)
    pack(1, mask_b, normed, send_b, rows_b)
    start_z(experts - 1)
    pack(2, mask_b, cot_b, send_c, rows_c)
    scores_b, share_b, whole_b = route(ids_b)

    def project(into, gate_w, up_w, half):
        lanes = pl.ds(half * hidden, hidden)

        def body(n, carry):
            cols = columns(n)
            part = into[:, :, :, cols].reshape(rows, cut)
            gate = dot(part, gate_w[cols, :])
            up = dot(part, up_w[cols, :])

            @pl.when(n == 0)
            def _():
                gate_s[:, lanes] = gate
                up_s[:, lanes] = up

            @pl.when(n > 0)
            def _():
                gate_s[:, lanes] += gate
                up_s[:, lanes] += up

            return carry

        lax.fori_loop(0, CHUNKS, body, 0)

    def grad_hidden(n, down_w, half):
        lanes = pl.ds(half * hidden, hidden)
        cols = columns(n)
        part = rows_c[:, :, :, cols].reshape(rows, cut)
        gact_s[:, lanes] += dot_last(part, down_w[:, cols])

    def activate(half):
        lanes = pl.ds(half * hidden, hidden)
        gate = gate_s[:, lanes]
        mid_a[:, lanes] = (gate * jax.nn.sigmoid(gate) * up_s[:, lanes]).astype(jnp.bfloat16)

    def prepare(half):
        lanes = pl.ds(half * hidden, hidden)
        gate = gate_s[:, lanes]
        up = up_s[:, lanes]
        sig = jax.nn.sigmoid(gate)
        swish = gate * sig
        mid_x[:, lanes] = (swish * up).astype(jnp.bfloat16)
        gate_s[:, lanes] = up * sig * (1.0 + gate * (1.0 - sig))
        up_s[:, lanes] = swish

    def finalize(half):
        lanes = pl.ds(half * hidden, hidden)
        gact = gact_s[:, lanes]
        mid_g[:, lanes] = (gact * gate_s[:, lanes]).astype(jnp.bfloat16)
        mid_u[:, lanes] = (gact * up_s[:, lanes]).astype(jnp.bfloat16)
        return jnp.sum(mid_x[:, lanes].astype(jnp.float32) * gact, axis=-1, keepdims=True)

    forward_blocks(0)
    for load in loads[3:]:
        load.wait()
    arrived(0, rows_a)
    project(rows_a, own_g, own_u, 0)
    activate(0)
    forward_blocks(1)
    down_copy(0).start()
    arrived(1, rows_b)
    project(rows_b, own_g, own_u, 0)
    prepare(0)
    forward_blocks(2)
    for n in range(1, AHEAD):
        down_copy(n).start()
    for copy in w_copies:
        copy.wait_recv()
    project(rows_a, oth_g, oth_u, 1)
    activate(1)
    gact_s[...] = jnp.zeros_like(gact_s)

    def yb_copy(i, n, source, into):
        return remote(source.at[n], into.at[n], yb_send.at[i, n], yb_recv.at[i, n], y_dev)

    def zb_copy(i, n, source, into, step):
        return remote(
            source.at[n, step],
            into.at[n, step],
            zb_send.at[i, n, step],
            zb_recv.at[i, n, step],
            behind(step),
        )

    def split_out(i, n, out, near, source, into):
        cols = columns(n)
        near[:total_slots, cols] = out[:total_slots]
        far = out[total_slots:].reshape(experts, slot, cut)
        source[n] = far.astype(jnp.bfloat16)
        yb_copy(i, n, source, into).start()

    def join(i, n, near, ysource, yinto, zsource, zinto):
        cols = columns(n)
        yb_copy(i, n, ysource, yinto).wait_recv()
        kept = near[:total_slots, cols].reshape(experts, slot, cut)
        summed = kept + yinto[n].astype(jnp.float32)
        summed = summed.astype(jnp.bfloat16)
        zsource[n] = summed
        zinto[n, 0] = summed[0]
        for step in range(1, experts):
            zb_copy(i, n, zsource, zinto, step).start()

    def start_down(n):
        down_copy(n).start()

    def down_step(n):
        cols = columns(n)
        down_copy(n).wait_recv()
        if not isinstance(n, int):
            pl.when(n + AHEAD < CHUNKS)(functools.partial(start_down, n + AHEAD))
        elif n + AHEAD < CHUNKS:
            start_down(n + AHEAD)
        out = dot(mid_a[:, :hidden], own_d[:, cols]) + dot(mid_a[:, hidden:], oth_d[:, cols])
        split_out(0, n, out, near_a, ysend_a, yback_a)

    def hidden_step(n):
        grad_hidden(n, oth_d, 1)
        grad_hidden(n, own_d, 0)

    def join_a(n):
        join(0, n, near_a, ysend_a, yback_a, zsend_a, home_a)

    def down_loop(n, carry):
        down_step(n)
        hidden_step(n)
        join_a(n - 1)
        return carry

    down_step(0)
    project(rows_b, oth_g, oth_u, 1)
    prepare(1)
    arrived(2, rows_c)
    hidden_step(0)
    lax.fori_loop(1, CHUNKS - 1, down_loop, 0)
    down_step(CHUNKS - 1)
    hidden_step(CHUNKS - 1)
    contract = jnp.broadcast_to(
        finalize(0) + finalize(1), (rows, LANES)
    )
    ysend_c[...] = contract[total_slots:].reshape(experts, slot, LANES).astype(jnp.bfloat16)
    near_c = contract[:total_slots].reshape(experts, slot, LANES)
    yc_copy = remote(ysend_c, yback_c, yb_send.at[1, CHUNKS], yb_recv.at[1, CHUNKS], y_dev)

    def zc_copy(step):
        return remote(
            zsend_c.at[step],
            home_c.at[step],
            zb_send.at[1, CHUNKS, step],
            zb_recv.at[1, CHUNKS, step],
            behind(step),
        )

    def grad_step(n):
        cols = columns(n)
        out = dot_last(mid_g[:, hidden:], oth_g[cols, :])
        out = out + dot_last(mid_u[:, hidden:], oth_u[cols, :])
        out = out + dot_last(mid_g[:, :hidden], own_g[cols, :])
        out = out + dot_last(mid_u[:, :hidden], own_u[cols, :])
        split_out(1, n, out, near_b, ysend_b, yback_b)

    def join_b(n):
        join(1, n, near_b, ysend_b, yback_b, zsend_b, home_b)

    grad_step(0)
    yc_copy.start()
    join_a(CHUNKS - 2)
    grad_step(1)
    join_a(CHUNKS - 1)
    join_b(0)
    yc_copy.wait_recv()
    summed_c = (near_c + yback_c[...].astype(jnp.float32)).astype(jnp.bfloat16)
    zsend_c[...] = summed_c
    home_c[0] = summed_c[0]
    for step in range(1, experts):
        zc_copy(step).start()

    def grad_loop(n, carry):
        grad_step(n)
        join_b(n - 1)
        return carry

    lax.fori_loop(2, CHUNKS, grad_loop, 0)
    join_b(CHUNKS - 1)

    def mix(i, n, zsource, zinto, masks, share):
        for step in range(1, experts):
            zb_copy(i, n, zsource, zinto, step).wait_recv()
        block = zinto[n].reshape(total_slots, cut)
        return functools.reduce(
            lambda a, b: a + b, [share[k] * dot(masks[k], block) for k in range(top)]
        )

    masks_a = unpack_masks(ids_a)

    def finish_a(n, carry):
        cols = columns(n)
        mixed = mix(0, n, zsend_a, home_a, masks_a, share_a)
        values = act_a[:, cols].astype(jnp.float32)
        sect_a[:, cols] = (values + route_scale * mixed).astype(jnp.bfloat16)
        return carry

    lax.fori_loop(0, CHUNKS, finish_a, 0)
    pa_copy = remote(sect_a, next_a, p_send.at[0], p_recv.at[0], next_pipe)
    pa_copy.start()

    masks_b = unpack_masks(ids_b)
    for step in range(1, experts):
        zc_copy(step).wait_recv()
    home = home_c[...].reshape(total_slots, LANES)
    grad_share = [route_scale * dot(masks_b[k], home)[:, :1] for k in range(top)]
    center = functools.reduce(
        lambda a, b: a + b, [share_b[k] * grad_share[k] for k in range(top)]
    )
    number = lax.broadcasted_iota(jnp.int32, (tokens, router.shape[0]), 1).astype(jnp.float32)
    dense = jnp.zeros((tokens, router.shape[0]), jnp.float32)
    for k in range(top):
        grad_score = (grad_share[k] - center) / whole_b
        grad_logit = grad_score * scores_b[k] * (1.0 - scores_b[k])
        dense = dense + jnp.where(ids_b[k] == number, grad_logit, 0.0)
    dense = dense.astype(jnp.bfloat16)

    def finish_b(n, inner):
        cols = columns(n)
        branch = mix(1, n, zsend_b, home_b, masks_b, share_b)
        term = dot(dense, router[:, cols])
        grad = (route_scale * branch + term) * gain[:, cols].astype(jnp.float32)
        grad_n[:, cols] = grad
        values = act_b[:, cols].astype(jnp.float32)
        return inner + jnp.sum(values * grad, axis=-1, keepdims=True)

    inner = lax.fori_loop(0, CHUNKS, finish_b, jnp.zeros((tokens, 1), jnp.float32))
    scale = inverse_b * inverse_b * inverse_b * (inner / width)

    def write_b(n, carry):
        cols = columns(n)
        values = act_b[:, cols].astype(jnp.float32)
        out = cot_b[:, cols].astype(jnp.float32) + inverse_b * grad_n[:, cols] - values * scale
        sect_b[:, cols] = out.astype(jnp.bfloat16)
        return carry

    lax.fori_loop(0, CHUNKS, write_b, 0)
    pb_copy = remote(sect_b, next_b, p_send.at[1], p_recv.at[1], last_pipe)
    pb_copy.start()

    for copy in w_copies:
        copy.wait_send()
    for i, into in enumerate((rows_a, rows_b, rows_c)):
        for step in range(experts):
            y_copy(i, into, step).wait_send()

    def drain(n, carry):
        down_copy(n).wait_send()
        yb_copy(0, n, ysend_a, yback_a).wait_send()
        yb_copy(1, n, ysend_b, yback_b).wait_send()
        for step in range(1, experts):
            zb_copy(0, n, zsend_a, home_a, step).wait_send()
            zb_copy(1, n, zsend_b, home_b, step).wait_send()
        return carry

    lax.fori_loop(0, CHUNKS, drain, 0)
    yc_copy.wait_send()
    for step in range(1, experts):
        zc_copy(step).wait_send()
    pa_copy.wait()
    pb_copy.wait()


def hand_out(from_a, from_b, into_a, into_b):
    into_a[...] = from_a[...]
    into_b[...] = from_b[...]


def per_device(act_a, ids_a, act_b, cot_b, ids_b, norm_gain, router, w_gate, w_up, w_down):
    n_expert = lax.axis_size("expert")
    n_pipe = lax.axis_size("pipe")
    experts = n_expert // SPLIT
    tokens, width = act_a.shape[1:]
    top = ids_a.shape[2]
    hidden = w_gate.shape[3]
    capacity = min(tokens, max(2, 5 * tokens * top // (4 * experts)))
    slot = -(-capacity // SLOT_ROWS) * SLOT_ROWS
    slots = experts * slot
    rows = 2 * slots
    sizes = (n_expert, n_pipe, experts, slot, top, width, hidden, tokens)

    def half(*dims):
        return pltpu.VMEM(dims, jnp.bfloat16)

    def full(*dims):
        return pltpu.VMEM(dims, jnp.float32)

    sem = pltpu.SemaphoreType.DMA
    block = (experts, slot, width)
    narrow = (experts, slot, LANES)
    pieces = (CHUNKS, experts, slot, width // CHUNKS)
    vmem = pl.BlockSpec(memory_space=pltpu.VMEM)
    anywhere = pl.BlockSpec(memory_space=pl.ANY)
    out = jax.ShapeDtypeStruct((tokens, width), jnp.bfloat16)
    next_a, next_b = pl.pallas_call(
        functools.partial(kernel, sizes),
        out_shape=(out, out),
        in_specs=[anywhere] * 3 + [vmem] * 4 + [anywhere] * 3,
        out_specs=(anywhere, anywhere),
        scratch_shapes=[
            half(width, hidden),
            half(width, hidden),
            half(hidden, width),
            half(width, hidden),
            half(width, hidden),
            half(hidden, width),
            half(tokens, width),
            half(tokens, width),
            half(tokens, width),
            half(tokens, width),
            half(*block),
            half(*block),
            half(*block),
            half(2, *block),
            half(2, *block),
            half(2, *block),
            full(rows, 2 * hidden),
            full(rows, 2 * hidden),
            full(rows, 2 * hidden),
            half(rows, 2 * hidden),
            half(rows, 2 * hidden),
            half(rows, 2 * hidden),
            half(rows, 2 * hidden),
            full(slots, width),
            full(slots, width),
            half(*pieces),
            half(*pieces),
            half(*narrow),
            half(*pieces),
            half(*pieces),
            half(*narrow),
            half(*pieces),
            half(*pieces),
            half(*narrow),
            half(*pieces),
            half(*pieces),
            half(*narrow),
            full(tokens, width),
            half(tokens, width),
            half(tokens, width),
            sem((6,)),
            sem((2 + CHUNKS,)),
            sem((2 + CHUNKS,)),
            sem((3, experts)),
            sem((3, experts)),
            sem((3, experts)),
            sem((3, experts)),
            sem((2, CHUNKS + 1)),
            sem((2, CHUNKS + 1)),
            sem((2, CHUNKS + 1, experts)),
            sem((2, CHUNKS + 1, experts)),
            sem((2,)),
            sem((2,)),
        ],
        compiler_params=pltpu.CompilerParams(
            collective_id=0, has_side_effects=True, vmem_limit_bytes=60 * 1024 * 1024
        ),
        cost_estimate=pl.CostEstimate(
            flops=2 * 9 * rows * width * hidden * 2,
            bytes_accessed=6 * width * hidden * 2,
            transcendentals=0,
        ),
    )(
        act_a[0],
        act_b[0],
        cot_b[0],
        ids_a[0].T,
        ids_b[0].T,
        norm_gain,
        router[0].T,
        w_gate[0, 0],
        w_up[0, 0],
        w_down[0, 0],
    )
    next_a, next_b = pl.pallas_call(
        hand_out,
        out_shape=(out, out),
        in_specs=[vmem] * 2,
        out_specs=(vmem, vmem),
    )(next_a, next_b)
    return (next_a[None], next_b[None])


SLOT_ROWS = 8


def solution(mesh):
    return jax.shard_map(
        per_device,
        mesh=mesh,
        in_specs=(
            P("pipe", "expert", None),
            P("pipe", "expert", None),
            P("pipe", "expert", None),
            P("pipe", "expert", None),
            P("pipe", "expert", None),
            P("pipe", None),
            P("pipe", None, None),
            P("pipe", "expert", None, None),
            P("pipe", "expert", None, None),
            P("pipe", "expert", None, None),
        ),
        out_specs=(P("pipe", "expert", None), P("pipe", "expert", None)),
        check_vma=False,
    )
```

```python
import functools
import jax
import jax.numpy as jnp
from jax import lax
from jax.experimental import pallas as pl
from jax.experimental.pallas import tpu as pltpu
from jax.sharding import PartitionSpec as P

SPLIT = 4
CHUNKS = 14
AHEAD = 8
PARTS = 7
LANES = 128
MESH = pl.DeviceIdType.MESH

route_scale = 2.5
norm_eps = 1e-06
last_dims = (((1,), (1,)), ((), ()))


def dot(left, right):
    return jnp.dot(left, right, preferred_element_type=jnp.float32)


def dot_last(left, right):
    return lax.dot_general(left, right, last_dims, preferred_element_type=jnp.float32)


def kernel(
    sizes,
    act_a_hbm,
    act_b_hbm,
    cot_b_hbm,
    idst_a,
    idst_b,
    gain,
    router,
    w_gate,
    w_up,
    w_down,
    next_a,
    next_b,
    own_g,
    own_u,
    own_d,
    oth_g,
    oth_u,
    oth_d,
    act_a,
    act_b,
    cot_b,
    normed,
    send_a,
    send_b,
    send_c,
    rows_a,
    rows_b,
    rows_c,
    gate_s,
    up_s,
    gact_s,
    mid_a,
    mid_g,
    mid_u,
    mid_x,
    near_a,
    near_b,
    ysend_a,
    ysend_b,
    ysend_c,
    yback_a,
    yback_b,
    yback_c,
    zsend_a,
    zsend_b,
    zsend_c,
    home_a,
    home_b,
    home_c,
    grad_n,
    sect_a,
    sect_b,
    load_sem,
    w_send,
    w_recv,
    z_send,
    z_recv,
    y_send,
    y_recv,
    yb_send,
    yb_recv,
    zb_send,
    zb_recv,
    p_send,
    p_recv,
):
    n_expert, n_pipe, experts, slot, top, width, hidden, tokens = sizes
    total_slots = experts * slot
    rows = 2 * total_slots
    cut = width // CHUNKS
    deep = width // PARTS
    me = lax.axis_index("expert")
    pipe = lax.axis_index("pipe")
    mine = me // SPLIT
    x_dev = {"expert": me + 1 - 2 * (me % 2)}
    y_dev = {"expert": me + 2 - 4 * ((me // 2) % 2)}

    def ahead(step):
        return {"expert": (me + SPLIT * step) % n_expert}

    def behind(step):
        return {"expert": (me + n_expert - SPLIT * step) % n_expert}

    next_pipe = {"pipe": (pipe + 1) % n_pipe}
    last_pipe = {"pipe": (pipe + n_pipe - 1) % n_pipe}

    def remote(src, dst, send, recv, device):
        return pltpu.make_async_remote_copy(
            src_ref=src,
            dst_ref=dst,
            send_sem=send,
            recv_sem=recv,
            device_id=device,
            device_id_type=MESH,
        )

    def columns(n):
        if isinstance(n, int):
            return pl.ds(n * cut, cut)
        return pl.ds(pl.multiple_of(n * cut, cut), cut)

    def wide(n):
        return pl.ds(pl.multiple_of(n * deep, deep), deep)

    loads = [
        pltpu.make_async_copy(src, dst, load_sem.at[i])
        for i, (src, dst) in enumerate(
            (
                (act_a_hbm, act_a),
                (act_b_hbm, act_b),
                (cot_b_hbm, cot_b),
                (w_gate, own_g),
                (w_up, own_u),
                (w_down, own_d),
            )
        )
    ]
    for load in loads:
        load.start()

    partners = [x_dev, y_dev] + [ahead(step) for step in range(1, experts)] + [next_pipe]
    if n_pipe > 2:
        partners.append(last_pipe)
    barrier = pltpu.get_barrier_semaphore()
    for partner in partners:
        pl.semaphore_signal(barrier, inc=1, device_id=partner, device_id_type=MESH)
    pl.semaphore_wait(barrier, len(partners))

    w_copies = [
        remote(w_gate, oth_g, w_send.at[0], w_recv.at[0], x_dev),
        remote(w_up, oth_u, w_send.at[1], w_recv.at[1], x_dev),
    ]

    def down_copy(n):
        cols = columns(n)
        return remote(
            w_down.at[:, cols], oth_d.at[:, cols], w_send.at[2 + n], w_recv.at[2 + n], x_dev
        )

    for copy in w_copies:
        copy.start()

    def z_copy(i, send, into, step):
        return remote(
            send.at[step], into.at[0, step], z_send.at[i, step], z_recv.at[i, step], ahead(step)
        )

    def y_copy(i, into, step):
        return remote(
            into.at[0, step], into.at[1, step], y_send.at[i, step], y_recv.at[i, step], y_dev
        )

    def block_of(index):
        count = jnp.zeros_like(index)
        for step in range(1, experts):
            count = count + jnp.where(index >= step * slot, 1, 0)
        place = (index - count * slot).astype(jnp.float32)
        expert = count + mine
        return jnp.where(expert >= experts, expert - experts, expert), place

    def ids_columns(idst):
        first = lax.broadcasted_iota(jnp.int32, (tokens, tokens), 0)
        second = lax.broadcasted_iota(jnp.int32, (tokens, tokens), 1)
        return [
            jnp.sum(
                jnp.where(first == second, idst[k : k + 1, :].astype(jnp.float32), 0.0),
                axis=1,
                keepdims=True,
            )
            for k in range(top)
        ]

    gain_row = gain[...].astype(jnp.float32)

    def normalize(act):
        values = act[...].astype(jnp.float32)
        inverse = lax.rsqrt(jnp.mean(values * values, axis=-1, keepdims=True) + norm_eps)
        normed[...] = (values * inverse * gain_row).astype(jnp.bfloat16)
        return inverse

    def route(ids):
        logits = dot_last(normed[...], router[...])
        number = lax.broadcasted_iota(jnp.int32, logits.shape, 1).astype(jnp.float32)
        scores = [
            jax.nn.sigmoid(
                jnp.sum(
                    jnp.where(ids[k] == number, logits, 0.0), axis=1, keepdims=True
                )
            )
            for k in range(top)
        ]
        whole = functools.reduce(lambda a, b: a + b, scores)
        return scores, [score / whole for score in scores], whole

    def pack_mask(idst):
        expert, place = block_of(lax.broadcasted_iota(jnp.int32, (total_slots, tokens), 0))
        named = jnp.zeros((total_slots, tokens), jnp.float32)
        for k in range(top):
            named = named + jnp.where(idst[k : k + 1, :] == expert, 1.0, 0.0)
        first = lax.broadcasted_iota(jnp.int32, (tokens, tokens), 0)
        second = lax.broadcasted_iota(jnp.int32, (tokens, tokens), 1)
        upper = jnp.where(first <= second, 1.0, 0.0).astype(jnp.bfloat16)
        count = dot(named.astype(jnp.bfloat16), upper)
        return jnp.where(count - 1.0 == place, named, 0.0).astype(jnp.bfloat16)

    def unpack_masks(ids):
        expert, place = block_of(lax.broadcasted_iota(jnp.int32, (tokens, total_slots), 1))
        expert = expert.astype(jnp.float32)
        hits = [jnp.where(ids[k] == expert, 1.0, 0.0) for k in range(top)]
        named = functools.reduce(lambda a, b: a + b, hits)
        first = lax.broadcasted_iota(jnp.int32, (tokens, tokens), 0)
        second = lax.broadcasted_iota(jnp.int32, (tokens, tokens), 1)
        lower = jnp.where(second <= first, 1.0, 0.0).astype(jnp.bfloat16)
        count = dot(lower, named.astype(jnp.bfloat16))
        return [jnp.where(count - 1.0 == place, hit, 0.0).astype(jnp.bfloat16) for hit in hits]

    def pack(i, mask, source, send, into):
        def body(n, carry):
            cols = wide(n)
            packed = dot(mask, source[:, cols]).reshape(experts, slot, deep).astype(jnp.bfloat16)
            send[:, :, cols] = packed
            into[0, 0, :, cols] = packed[0]
            return carry

        lax.fori_loop(0, PARTS, body, 0)

    arrays = ((send_a, rows_a), (send_b, rows_b), (send_c, rows_c))
    order = [(i, step) for i in range(3) for step in range(1, experts)]

    def start_z(place):
        if place < len(order):
            i, step = order[place]
            z_copy(i, *arrays[i], step).start()

    def forward_blocks(i):
        for step in range(1, experts):
            z_copy(i, *arrays[i], step).wait_recv()
            y_copy(i, arrays[i][1], step).start()
            z_copy(i, *arrays[i], step).wait_send()
            start_z(order.index((i, step)) + experts)
        if i < 2:
            y_copy(i + 1, arrays[i + 1][1], 0).start()

    def arrived(i, into):
        for step in range(experts):
            y_copy(i, into, step).wait_recv()

    ids_a = ids_columns(idst_a)
    ids_b = ids_columns(idst_b)
    for load in loads[:3]:
        load.wait()
    inverse_a = normalize(act_a)
    share_a = route(ids_a)[1]
    pack(0, pack_mask(idst_a), normed, send_a, rows_a)
    for place in range(experts - 1):
        start_z(place)
    y_copy(0, rows_a, 0).start()
    inverse_b = normalize(act_b)
    mask_b = pack_mask(idst_b)
    pack(1, mask_b, normed, send_b, rows_b)
    start_z(experts - 1)
    pack(2, mask_b, cot_b, send_c, rows_c)
    scores_b, share_b, whole_b = route(ids_b)

    def project(into, gate_w, up_w, half):
        lanes = pl.ds(half * hidden, hidden)

        def body(n, carry):
            cols = wide(n)
            part = into[:, :, :, cols].reshape(rows, deep)
            gate = dot(part, gate_w[cols, :])
            up = dot(part, up_w[cols, :])

            @pl.when(n == 0)
            def _():
                gate_s[:, lanes] = gate
                up_s[:, lanes] = up

            @pl.when(n > 0)
            def _():
                gate_s[:, lanes] += gate
                up_s[:, lanes] += up

            return carry

        lax.fori_loop(0, PARTS, body, 0)

    def grad_hidden(n, down_w, half):
        lanes = pl.ds(half * hidden, hidden)
        cols = columns(n)
        part = rows_c[:, :, :, cols].reshape(rows, cut)
        gact_s[:, lanes] += dot_last(part, down_w[:, cols])

    def activate(half):
        lanes = pl.ds(half * hidden, hidden)
        gate = gate_s[:, lanes]
        mid_a[:, lanes] = (gate * jax.nn.sigmoid(gate) * up_s[:, lanes]).astype(jnp.bfloat16)

    def prepare(half):
        lanes = pl.ds(half * hidden, hidden)
        gate = gate_s[:, lanes]
        up = up_s[:, lanes]
        sig = jax.nn.sigmoid(gate)
        swish = gate * sig
        mid_x[:, lanes] = (swish * up).astype(jnp.bfloat16)
        gate_s[:, lanes] = up * sig * (1.0 + gate * (1.0 - sig))
        up_s[:, lanes] = swish

    def finalize(half):
        lanes = pl.ds(half * hidden, hidden)
        gact = gact_s[:, lanes]
        mid_g[:, lanes] = (gact * gate_s[:, lanes]).astype(jnp.bfloat16)
        mid_u[:, lanes] = (gact * up_s[:, lanes]).astype(jnp.bfloat16)
        return jnp.sum(mid_x[:, lanes].astype(jnp.float32) * gact, axis=-1, keepdims=True)

    forward_blocks(0)
    for load in loads[3:]:
        load.wait()
    arrived(0, rows_a)
    project(rows_a, own_g, own_u, 0)
    activate(0)
    forward_blocks(1)
    for n in range(2):
        down_copy(n).start()
    arrived(1, rows_b)
    project(rows_b, own_g, own_u, 0)
    prepare(0)
    forward_blocks(2)
    for n in range(2, AHEAD):
        down_copy(n).start()
    for copy in w_copies:
        copy.wait_recv()
    project(rows_a, oth_g, oth_u, 1)
    activate(1)
    gact_s[...] = jnp.zeros_like(gact_s)

    def yb_copy(i, n, source, into):
        return remote(source.at[n], into.at[n], yb_send.at[i, n], yb_recv.at[i, n], y_dev)

    def zb_copy(i, n, source, into, step):
        return remote(
            source.at[n, step],
            into.at[n, step],
            zb_send.at[i, n, step],
            zb_recv.at[i, n, step],
            behind(step),
        )

    def split_out(i, n, out, near, source, into):
        cols = columns(n)
        near[:total_slots, cols] = out[:total_slots]
        far = out[total_slots:].reshape(experts, slot, cut)
        source[n] = far.astype(jnp.bfloat16)
        yb_copy(i, n, source, into).start()

    def join(i, n, near, ysource, yinto, zsource, zinto):
        cols = columns(n)
        yb_copy(i, n, ysource, yinto).wait_recv()
        kept = near[:total_slots, cols].reshape(experts, slot, cut)
        summed = kept + yinto[n].astype(jnp.float32)
        summed = summed.astype(jnp.bfloat16)
        zsource[n] = summed
        zinto[n, 0] = summed[0]
        for step in range(1, experts):
            zb_copy(i, n, zsource, zinto, step).start()

    def start_down(n):
        down_copy(n).start()

    def down_step(n):
        cols = columns(n)
        down_copy(n).wait_recv()
        if not isinstance(n, int):
            pl.when(n + AHEAD < CHUNKS)(functools.partial(start_down, n + AHEAD))
        elif n + AHEAD < CHUNKS:
            start_down(n + AHEAD)
        out = dot(mid_a[:, :hidden], own_d[:, cols]) + dot(mid_a[:, hidden:], oth_d[:, cols])
        split_out(0, n, out, near_a, ysend_a, yback_a)

    def hidden_step(n):
        grad_hidden(n, oth_d, 1)
        grad_hidden(n, own_d, 0)

    def join_a(n):
        join(0, n, near_a, ysend_a, yback_a, zsend_a, home_a)

    def down_loop(n, carry):
        down_step(n)
        hidden_step(n)
        join_a(n - 1)
        return carry

    down_step(0)
    project(rows_b, oth_g, oth_u, 1)
    prepare(1)
    arrived(2, rows_c)
    hidden_step(0)
    lax.fori_loop(1, CHUNKS - 1, down_loop, 0)
    down_step(CHUNKS - 1)
    hidden_step(CHUNKS - 1)
    contract = jnp.broadcast_to(
        finalize(0) + finalize(1), (rows, LANES)
    )
    ysend_c[...] = contract[total_slots:].reshape(experts, slot, LANES).astype(jnp.bfloat16)
    near_c = contract[:total_slots].reshape(experts, slot, LANES)
    yc_copy = remote(ysend_c, yback_c, yb_send.at[1, CHUNKS], yb_recv.at[1, CHUNKS], y_dev)

    def zc_copy(step):
        return remote(
            zsend_c.at[step],
            home_c.at[step],
            zb_send.at[1, CHUNKS, step],
            zb_recv.at[1, CHUNKS, step],
            behind(step),
        )

    def grad_step(n):
        cols = columns(n)
        out = dot_last(mid_g[:, hidden:], oth_g[cols, :])
        out = out + dot_last(mid_u[:, hidden:], oth_u[cols, :])
        out = out + dot_last(mid_g[:, :hidden], own_g[cols, :])
        out = out + dot_last(mid_u[:, :hidden], own_u[cols, :])
        split_out(1, n, out, near_b, ysend_b, yback_b)

    def join_b(n):
        join(1, n, near_b, ysend_b, yback_b, zsend_b, home_b)

    grad_step(0)
    yc_copy.start()
    join_a(CHUNKS - 2)
    grad_step(1)
    join_a(CHUNKS - 1)
    join_b(0)
    yc_copy.wait_recv()
    summed_c = (near_c + yback_c[...].astype(jnp.float32)).astype(jnp.bfloat16)
    zsend_c[...] = summed_c
    home_c[0] = summed_c[0]
    for step in range(1, experts):
        zc_copy(step).start()

    def grad_loop(n, carry):
        grad_step(n)
        join_b(n - 1)
        return carry

    lax.fori_loop(2, CHUNKS, grad_loop, 0)
    join_b(CHUNKS - 1)

    def mix(i, n, zsource, zinto, masks, share):
        for step in range(1, experts):
            zb_copy(i, n, zsource, zinto, step).wait_recv()
        block = zinto[n].reshape(total_slots, cut)
        return functools.reduce(
            lambda a, b: a + b, [share[k] * dot(masks[k], block) for k in range(top)]
        )

    masks_a = unpack_masks(ids_a)

    def finish_a(n, carry):
        cols = columns(n)
        mixed = mix(0, n, zsend_a, home_a, masks_a, share_a)
        values = act_a[:, cols].astype(jnp.float32)
        sect_a[:, cols] = (values + route_scale * mixed).astype(jnp.bfloat16)
        return carry

    lax.fori_loop(0, CHUNKS, finish_a, 0)
    pa_copy = remote(sect_a, next_a, p_send.at[0], p_recv.at[0], next_pipe)
    pa_copy.start()

    masks_b = unpack_masks(ids_b)
    for step in range(1, experts):
        zc_copy(step).wait_recv()
    home = home_c[...].reshape(total_slots, LANES)
    grad_share = [route_scale * dot(masks_b[k], home)[:, :1] for k in range(top)]
    center = functools.reduce(
        lambda a, b: a + b, [share_b[k] * grad_share[k] for k in range(top)]
    )
    number = lax.broadcasted_iota(jnp.int32, (tokens, router.shape[0]), 1).astype(jnp.float32)
    dense = jnp.zeros((tokens, router.shape[0]), jnp.float32)
    for k in range(top):
        grad_score = (grad_share[k] - center) / whole_b
        grad_logit = grad_score * scores_b[k] * (1.0 - scores_b[k])
        dense = dense + jnp.where(ids_b[k] == number, grad_logit, 0.0)
    dense = dense.astype(jnp.bfloat16)

    def finish_b(n, inner):
        cols = columns(n)
        branch = mix(1, n, zsend_b, home_b, masks_b, share_b)
        term = dot(dense, router[:, cols])
        grad = (route_scale * branch + term) * gain[:, cols].astype(jnp.float32)
        grad_n[:, cols] = grad
        values = act_b[:, cols].astype(jnp.float32)
        return inner + jnp.sum(values * grad, axis=-1, keepdims=True)

    inner = lax.fori_loop(0, CHUNKS, finish_b, jnp.zeros((tokens, 1), jnp.float32))
    scale = inverse_b * inverse_b * inverse_b * (inner / width)

    def write_b(n, carry):
        cols = columns(n)
        values = act_b[:, cols].astype(jnp.float32)
        out = cot_b[:, cols].astype(jnp.float32) + inverse_b * grad_n[:, cols] - values * scale
        sect_b[:, cols] = out.astype(jnp.bfloat16)
        return carry

    lax.fori_loop(0, CHUNKS, write_b, 0)
    pb_copy = remote(sect_b, next_b, p_send.at[1], p_recv.at[1], last_pipe)
    pb_copy.start()

    for copy in w_copies:
        copy.wait_send()
    for i, into in enumerate((rows_a, rows_b, rows_c)):
        for step in range(experts):
            y_copy(i, into, step).wait_send()

    def drain(n, carry):
        down_copy(n).wait_send()
        yb_copy(0, n, ysend_a, yback_a).wait_send()
        yb_copy(1, n, ysend_b, yback_b).wait_send()
        for step in range(1, experts):
            zb_copy(0, n, zsend_a, home_a, step).wait_send()
            zb_copy(1, n, zsend_b, home_b, step).wait_send()
        return carry

    lax.fori_loop(0, CHUNKS, drain, 0)
    yc_copy.wait_send()
    for step in range(1, experts):
        zc_copy(step).wait_send()
    pa_copy.wait()
    pb_copy.wait()


def hand_out(from_a, from_b, into_a, into_b):
    into_a[...] = from_a[...]
    into_b[...] = from_b[...]


def per_device(act_a, ids_a, act_b, cot_b, ids_b, norm_gain, router, w_gate, w_up, w_down):
    n_expert = lax.axis_size("expert")
    n_pipe = lax.axis_size("pipe")
    experts = n_expert // SPLIT
    tokens, width = act_a.shape[1:]
    top = ids_a.shape[2]
    hidden = w_gate.shape[3]
    capacity = min(tokens, max(2, 5 * tokens * top // (4 * experts)))
    slot = -(-capacity // SLOT_ROWS) * SLOT_ROWS
    slots = experts * slot
    rows = 2 * slots
    sizes = (n_expert, n_pipe, experts, slot, top, width, hidden, tokens)

    def half(*dims):
        return pltpu.VMEM(dims, jnp.bfloat16)

    def full(*dims):
        return pltpu.VMEM(dims, jnp.float32)

    sem = pltpu.SemaphoreType.DMA
    block = (experts, slot, width)
    narrow = (experts, slot, LANES)
    pieces = (CHUNKS, experts, slot, width // CHUNKS)
    vmem = pl.BlockSpec(memory_space=pltpu.VMEM)
    anywhere = pl.BlockSpec(memory_space=pl.ANY)
    out = jax.ShapeDtypeStruct((tokens, width), jnp.bfloat16)
    next_a, next_b = pl.pallas_call(
        functools.partial(kernel, sizes),
        out_shape=(out, out),
        in_specs=[anywhere] * 3 + [vmem] * 4 + [anywhere] * 3,
        out_specs=(anywhere, anywhere),
        scratch_shapes=[
            half(width, hidden),
            half(width, hidden),
            half(hidden, width),
            half(width, hidden),
            half(width, hidden),
            half(hidden, width),
            half(tokens, width),
            half(tokens, width),
            half(tokens, width),
            half(tokens, width),
            half(*block),
            half(*block),
            half(*block),
            half(2, *block),
            half(2, *block),
            half(2, *block),
            full(rows, 2 * hidden),
            full(rows, 2 * hidden),
            full(rows, 2 * hidden),
            half(rows, 2 * hidden),
            half(rows, 2 * hidden),
            half(rows, 2 * hidden),
            half(rows, 2 * hidden),
            full(slots, width),
            full(slots, width),
            half(*pieces),
            half(*pieces),
            half(*narrow),
            half(*pieces),
            half(*pieces),
            half(*narrow),
            half(*pieces),
            half(*pieces),
            half(*narrow),
            half(*pieces),
            half(*pieces),
            half(*narrow),
            full(tokens, width),
            half(tokens, width),
            half(tokens, width),
            sem((6,)),
            sem((2 + CHUNKS,)),
            sem((2 + CHUNKS,)),
            sem((3, experts)),
            sem((3, experts)),
            sem((3, experts)),
            sem((3, experts)),
            sem((2, CHUNKS + 1)),
            sem((2, CHUNKS + 1)),
            sem((2, CHUNKS + 1, experts)),
            sem((2, CHUNKS + 1, experts)),
            sem((2,)),
            sem((2,)),
        ],
        compiler_params=pltpu.CompilerParams(
            collective_id=0, has_side_effects=True, vmem_limit_bytes=60 * 1024 * 1024
        ),
        cost_estimate=pl.CostEstimate(
            flops=2 * 9 * rows * width * hidden * 2,
            bytes_accessed=6 * width * hidden * 2,
            transcendentals=0,
        ),
    )(
        act_a[0],
        act_b[0],
        cot_b[0],
        ids_a[0].T,
        ids_b[0].T,
        norm_gain,
        router[0].T,
        w_gate[0, 0],
        w_up[0, 0],
        w_down[0, 0],
    )
    next_a, next_b = pl.pallas_call(
        hand_out,
        out_shape=(out, out),
        in_specs=[vmem] * 2,
        out_specs=(vmem, vmem),
    )(next_a, next_b)
    return (next_a[None], next_b[None])


SLOT_ROWS = 8


def solution(mesh):
    return jax.shard_map(
        per_device,
        mesh=mesh,
        in_specs=(
            P("pipe", "expert", None),
            P("pipe", "expert", None),
            P("pipe", "expert", None),
            P("pipe", "expert", None),
            P("pipe", "expert", None),
            P("pipe", None),
            P("pipe", None, None),
            P("pipe", "expert", None, None),
            P("pipe", "expert", None, None),
            P("pipe", "expert", None, None),
        ),
        out_specs=(P("pipe", "expert", None), P("pipe", "expert", None)),
        check_vma=False,
    )
```

```python
import functools
import jax
import jax.numpy as jnp
from jax import lax
from jax.experimental import pallas as pl
from jax.experimental.pallas import tpu as pltpu
from jax.sharding import PartitionSpec as P

SPLIT = 4
CHUNKS = 7
AHEAD = 4
LANES = 128
MESH = pl.DeviceIdType.MESH

route_scale = 2.5
norm_eps = 1e-06
last_dims = (((1,), (1,)), ((), ()))


def dot(left, right):
    return jnp.dot(left, right, preferred_element_type=jnp.float32)


def dot_last(left, right):
    return lax.dot_general(left, right, last_dims, preferred_element_type=jnp.float32)


def kernel(
    sizes,
    act_a_hbm,
    act_b_hbm,
    cot_b_hbm,
    idst_a,
    idst_b,
    gain,
    router,
    w_gate,
    w_up,
    w_down,
    next_a,
    next_b,
    own_g,
    own_u,
    own_d,
    oth_g,
    oth_u,
    oth_d,
    act_a,
    act_b,
    cot_b,
    normed,
    send_a,
    send_b,
    send_c,
    rows_a,
    rows_b,
    rows_c,
    gate_s,
    up_s,
    gact_s,
    mid_a,
    mid_g,
    mid_u,
    mid_x,
    near_a,
    near_b,
    ysend_a,
    ysend_b,
    ysend_c,
    yback_a,
    yback_b,
    yback_c,
    zsend_a,
    zsend_b,
    zsend_c,
    home_a,
    home_b,
    home_c,
    grad_n,
    sect_a,
    sect_b,
    load_sem,
    w_send,
    w_recv,
    z_send,
    z_recv,
    y_send,
    y_recv,
    yb_send,
    yb_recv,
    zb_send,
    zb_recv,
    p_send,
    p_recv,
):
    n_expert, n_pipe, experts, slot, top, width, hidden, tokens = sizes
    total_slots = experts * slot
    rows = 2 * total_slots
    cut = width // CHUNKS
    me = lax.axis_index("expert")
    pipe = lax.axis_index("pipe")
    mine = me // SPLIT
    x_dev = {"expert": me + 1 - 2 * (me % 2)}
    y_dev = {"expert": me + 2 - 4 * ((me // 2) % 2)}

    def ahead(step):
        return {"expert": (me + SPLIT * step) % n_expert}

    def behind(step):
        return {"expert": (me + n_expert - SPLIT * step) % n_expert}

    next_pipe = {"pipe": (pipe + 1) % n_pipe}
    last_pipe = {"pipe": (pipe + n_pipe - 1) % n_pipe}

    def remote(src, dst, send, recv, device):
        return pltpu.make_async_remote_copy(
            src_ref=src,
            dst_ref=dst,
            send_sem=send,
            recv_sem=recv,
            device_id=device,
            device_id_type=MESH,
        )

    def columns(n):
        if isinstance(n, int):
            return pl.ds(n * cut, cut)
        return pl.ds(pl.multiple_of(n * cut, cut), cut)

    loads = [
        pltpu.make_async_copy(src, dst, load_sem.at[i])
        for i, (src, dst) in enumerate(
            (
                (act_a_hbm, act_a),
                (act_b_hbm, act_b),
                (cot_b_hbm, cot_b),
                (w_gate, own_g),
                (w_up, own_u),
                (w_down, own_d),
            )
        )
    ]
    for load in loads:
        load.start()

    partners = [x_dev, y_dev] + [ahead(step) for step in range(1, experts)] + [next_pipe]
    if n_pipe > 2:
        partners.append(last_pipe)
    barrier = pltpu.get_barrier_semaphore()
    for partner in partners:
        pl.semaphore_signal(barrier, inc=1, device_id=partner, device_id_type=MESH)
    pl.semaphore_wait(barrier, len(partners))

    w_copies = [
        remote(w_gate, oth_g, w_send.at[0], w_recv.at[0], x_dev),
        remote(w_up, oth_u, w_send.at[1], w_recv.at[1], x_dev),
    ]

    def down_copy(n):
        cols = columns(n)
        return remote(
            w_down.at[:, cols], oth_d.at[:, cols], w_send.at[2 + n], w_recv.at[2 + n], x_dev
        )

    for copy in w_copies:
        copy.start()

    def z_copy(i, send, into, step):
        return remote(
            send.at[step], into.at[0, step], z_send.at[i, step], z_recv.at[i, step], ahead(step)
        )

    def y_copy(i, into, step):
        return remote(
            into.at[0, step], into.at[1, step], y_send.at[i, step], y_recv.at[i, step], y_dev
        )

    def block_of(index):
        count = jnp.zeros_like(index)
        for step in range(1, experts):
            count = count + jnp.where(index >= step * slot, 1, 0)
        place = (index - count * slot).astype(jnp.float32)
        expert = count + mine
        return jnp.where(expert >= experts, expert - experts, expert), place

    def ids_columns(idst):
        first = lax.broadcasted_iota(jnp.int32, (tokens, tokens), 0)
        second = lax.broadcasted_iota(jnp.int32, (tokens, tokens), 1)
        return [
            jnp.sum(
                jnp.where(first == second, idst[k : k + 1, :].astype(jnp.float32), 0.0),
                axis=1,
                keepdims=True,
            )
            for k in range(top)
        ]

    gain_row = gain[...].astype(jnp.float32)

    def normalize(act):
        values = act[...].astype(jnp.float32)
        inverse = lax.rsqrt(jnp.mean(values * values, axis=-1, keepdims=True) + norm_eps)
        normed[...] = (values * inverse * gain_row).astype(jnp.bfloat16)
        return inverse

    def route(ids):
        logits = dot_last(normed[...], router[...])
        number = lax.broadcasted_iota(jnp.int32, logits.shape, 1).astype(jnp.float32)
        scores = [
            jax.nn.sigmoid(
                jnp.sum(
                    jnp.where(ids[k] == number, logits, 0.0), axis=1, keepdims=True
                )
            )
            for k in range(top)
        ]
        whole = functools.reduce(lambda a, b: a + b, scores)
        return scores, [score / whole for score in scores], whole

    def pack_mask(idst):
        expert, place = block_of(lax.broadcasted_iota(jnp.int32, (total_slots, tokens), 0))
        named = jnp.zeros((total_slots, tokens), jnp.float32)
        for k in range(top):
            named = named + jnp.where(idst[k : k + 1, :] == expert, 1.0, 0.0)
        first = lax.broadcasted_iota(jnp.int32, (tokens, tokens), 0)
        second = lax.broadcasted_iota(jnp.int32, (tokens, tokens), 1)
        upper = jnp.where(first <= second, 1.0, 0.0).astype(jnp.bfloat16)
        count = dot(named.astype(jnp.bfloat16), upper)
        return jnp.where(count - 1.0 == place, named, 0.0).astype(jnp.bfloat16)

    def unpack_masks(ids):
        expert, place = block_of(lax.broadcasted_iota(jnp.int32, (tokens, total_slots), 1))
        expert = expert.astype(jnp.float32)
        hits = [jnp.where(ids[k] == expert, 1.0, 0.0) for k in range(top)]
        named = functools.reduce(lambda a, b: a + b, hits)
        first = lax.broadcasted_iota(jnp.int32, (tokens, tokens), 0)
        second = lax.broadcasted_iota(jnp.int32, (tokens, tokens), 1)
        lower = jnp.where(second <= first, 1.0, 0.0).astype(jnp.bfloat16)
        count = dot(lower, named.astype(jnp.bfloat16))
        return [jnp.where(count - 1.0 == place, hit, 0.0).astype(jnp.bfloat16) for hit in hits]

    def pack(i, mask, source, send, into):
        def body(n, carry):
            cols = columns(n)
            packed = dot(mask, source[:, cols]).reshape(experts, slot, cut).astype(jnp.bfloat16)
            send[:, :, cols] = packed
            into[0, 0, :, cols] = packed[0]
            return carry

        lax.fori_loop(0, CHUNKS, body, 0)

    arrays = ((send_a, rows_a), (send_b, rows_b), (send_c, rows_c))
    order = [(i, step) for i in range(3) for step in range(1, experts)]

    def start_z(place):
        if place < len(order):
            i, step = order[place]
            z_copy(i, *arrays[i], step).start()

    def forward_blocks(i):
        for step in range(1, experts):
            z_copy(i, *arrays[i], step).wait_recv()
            y_copy(i, arrays[i][1], step).start()
            z_copy(i, *arrays[i], step).wait_send()
            start_z(order.index((i, step)) + experts)
        if i < 2:
            y_copy(i + 1, arrays[i + 1][1], 0).start()

    def arrived(i, into):
        for step in range(experts):
            y_copy(i, into, step).wait_recv()

    ids_a = ids_columns(idst_a)
    ids_b = ids_columns(idst_b)
    for load in loads[:3]:
        load.wait()
    inverse_a = normalize(act_a)
    share_a = route(ids_a)[1]
    pack(0, pack_mask(idst_a), normed, send_a, rows_a)
    for place in range(experts - 1):
        start_z(place)
    y_copy(0, rows_a, 0).start()
    inverse_b = normalize(act_b)
    mask_b = pack_mask(idst_b)
    pack(1, mask_b, normed, send_b, rows_b)
    start_z(experts - 1)
    pack(2, mask_b, cot_b, send_c, rows_c)
    scores_b, share_b, whole_b = route(ids_b)

    def project(into, gate_w, up_w, half):
        lanes = pl.ds(half * hidden, hidden)

        def body(n, carry):
            cols = columns(n)
            part = into[:, :, :, cols].reshape(rows, cut)
            gate = dot(part, gate_w[cols, :])
            up = dot(part, up_w[cols, :])

            @pl.when(n == 0)
            def _():
                gate_s[:, lanes] = gate
                up_s[:, lanes] = up

            @pl.when(n > 0)
            def _():
                gate_s[:, lanes] += gate
                up_s[:, lanes] += up

            return carry

        lax.fori_loop(0, CHUNKS, body, 0)

    def grad_hidden(n, down_w, half):
        lanes = pl.ds(half * hidden, hidden)
        cols = columns(n)
        part = rows_c[:, :, :, cols].reshape(rows, cut)
        gact_s[:, lanes] += dot_last(part, down_w[:, cols])

    def activate(half):
        lanes = pl.ds(half * hidden, hidden)
        gate = gate_s[:, lanes]
        mid_a[:, lanes] = (gate * jax.nn.sigmoid(gate) * up_s[:, lanes]).astype(jnp.bfloat16)

    def prepare(half):
        lanes = pl.ds(half * hidden, hidden)
        gate = gate_s[:, lanes]
        up = up_s[:, lanes]
        sig = jax.nn.sigmoid(gate)
        swish = gate * sig
        mid_x[:, lanes] = (swish * up).astype(jnp.bfloat16)
        gate_s[:, lanes] = up * sig * (1.0 + gate * (1.0 - sig))
        up_s[:, lanes] = swish

    def finalize(half):
        lanes = pl.ds(half * hidden, hidden)
        gact = gact_s[:, lanes]
        mid_g[:, lanes] = (gact * gate_s[:, lanes]).astype(jnp.bfloat16)
        mid_u[:, lanes] = (gact * up_s[:, lanes]).astype(jnp.bfloat16)
        return jnp.sum(mid_x[:, lanes].astype(jnp.float32) * gact, axis=-1, keepdims=True)

    forward_blocks(0)
    for load in loads[3:]:
        load.wait()
    arrived(0, rows_a)
    project(rows_a, own_g, own_u, 0)
    activate(0)
    forward_blocks(1)
    down_copy(0).start()
    arrived(1, rows_b)
    project(rows_b, own_g, own_u, 0)
    prepare(0)
    forward_blocks(2)
    for n in range(1, AHEAD):
        down_copy(n).start()
    for copy in w_copies:
        copy.wait_recv()
    project(rows_a, oth_g, oth_u, 1)
    activate(1)
    gact_s[...] = jnp.zeros_like(gact_s)

    def yb_copy(i, n, source, into):
        return remote(source.at[n], into.at[n], yb_send.at[i, n], yb_recv.at[i, n], y_dev)

    def zb_copy(i, n, source, into, step):
        return remote(
            source.at[n, step],
            into.at[n, step],
            zb_send.at[i, n, step],
            zb_recv.at[i, n, step],
            behind(step),
        )

    def split_out(i, n, out, near, source, into):
        cols = columns(n)
        near[:total_slots, cols] = out[:total_slots]
        far = out[total_slots:].reshape(experts, slot, cut)
        source[n] = far.astype(jnp.bfloat16)
        yb_copy(i, n, source, into).start()

    def join(i, n, near, ysource, yinto, zsource, zinto):
        cols = columns(n)
        yb_copy(i, n, ysource, yinto).wait_recv()
        kept = near[:total_slots, cols].reshape(experts, slot, cut)
        summed = kept + yinto[n].astype(jnp.float32)
        summed = summed.astype(jnp.bfloat16)
        zsource[n] = summed
        zinto[n, 0] = summed[0]
        for step in range(1, experts):
            zb_copy(i, n, zsource, zinto, step).start()

    def start_down(n):
        down_copy(n).start()

    def down_step(n):
        cols = columns(n)
        down_copy(n).wait_recv()
        if not isinstance(n, int):
            pl.when(n + AHEAD < CHUNKS)(functools.partial(start_down, n + AHEAD))
        elif n + AHEAD < CHUNKS:
            start_down(n + AHEAD)
        out = dot(mid_a[:, :hidden], own_d[:, cols]) + dot(mid_a[:, hidden:], oth_d[:, cols])
        split_out(0, n, out, near_a, ysend_a, yback_a)

    def hidden_step(n):
        grad_hidden(n, oth_d, 1)
        grad_hidden(n, own_d, 0)

    def join_a(n):
        join(0, n, near_a, ysend_a, yback_a, zsend_a, home_a)

    def down_loop(n, carry):
        down_step(n)
        hidden_step(n)
        join_a(n - 1)
        return carry

    down_step(0)
    project(rows_b, oth_g, oth_u, 1)
    prepare(1)
    arrived(2, rows_c)
    hidden_step(0)
    lax.fori_loop(1, CHUNKS - 1, down_loop, 0)
    down_step(CHUNKS - 1)
    hidden_step(CHUNKS - 1)
    contract = jnp.broadcast_to(
        finalize(0) + finalize(1), (rows, LANES)
    )
    ysend_c[...] = contract[total_slots:].reshape(experts, slot, LANES).astype(jnp.bfloat16)
    near_c = contract[:total_slots].reshape(experts, slot, LANES)
    yc_copy = remote(ysend_c, yback_c, yb_send.at[1, CHUNKS], yb_recv.at[1, CHUNKS], y_dev)

    def zc_copy(step):
        return remote(
            zsend_c.at[step],
            home_c.at[step],
            zb_send.at[1, CHUNKS, step],
            zb_recv.at[1, CHUNKS, step],
            behind(step),
        )

    def grad_step(n):
        cols = columns(n)
        out = dot_last(mid_g[:, hidden:], oth_g[cols, :])
        out = out + dot_last(mid_u[:, hidden:], oth_u[cols, :])
        out = out + dot_last(mid_g[:, :hidden], own_g[cols, :])
        out = out + dot_last(mid_u[:, :hidden], own_u[cols, :])
        split_out(1, n, out, near_b, ysend_b, yback_b)

    def join_b(n):
        join(1, n, near_b, ysend_b, yback_b, zsend_b, home_b)

    grad_step(0)
    yc_copy.start()
    join_a(CHUNKS - 2)
    grad_step(1)
    join_a(CHUNKS - 1)
    grad_step(2)
    join_b(0)
    yc_copy.wait_recv()
    summed_c = (near_c + yback_c[...].astype(jnp.float32)).astype(jnp.bfloat16)
    zsend_c[...] = summed_c
    home_c[0] = summed_c[0]
    for step in range(1, experts):
        zc_copy(step).start()

    def grad_loop(n, carry):
        grad_step(n)
        join_b(n - 2)
        return carry

    lax.fori_loop(3, CHUNKS, grad_loop, 0)
    join_b(CHUNKS - 2)
    join_b(CHUNKS - 1)

    def mix(i, n, zsource, zinto, masks, share):
        for step in range(1, experts):
            zb_copy(i, n, zsource, zinto, step).wait_recv()
        block = zinto[n].reshape(total_slots, cut)
        return functools.reduce(
            lambda a, b: a + b, [share[k] * dot(masks[k], block) for k in range(top)]
        )

    masks_a = unpack_masks(ids_a)

    def finish_a(n, carry):
        cols = columns(n)
        mixed = mix(0, n, zsend_a, home_a, masks_a, share_a)
        values = act_a[:, cols].astype(jnp.float32)
        sect_a[:, cols] = (values + route_scale * mixed).astype(jnp.bfloat16)
        return carry

    lax.fori_loop(0, CHUNKS, finish_a, 0)
    pa_copy = remote(sect_a, next_a, p_send.at[0], p_recv.at[0], next_pipe)
    pa_copy.start()

    masks_b = unpack_masks(ids_b)
    for step in range(1, experts):
        zc_copy(step).wait_recv()
    home = home_c[...].reshape(total_slots, LANES)
    grad_share = [route_scale * dot(masks_b[k], home)[:, :1] for k in range(top)]
    center = functools.reduce(
        lambda a, b: a + b, [share_b[k] * grad_share[k] for k in range(top)]
    )
    number = lax.broadcasted_iota(jnp.int32, (tokens, router.shape[0]), 1).astype(jnp.float32)
    dense = jnp.zeros((tokens, router.shape[0]), jnp.float32)
    for k in range(top):
        grad_score = (grad_share[k] - center) / whole_b
        grad_logit = grad_score * scores_b[k] * (1.0 - scores_b[k])
        dense = dense + jnp.where(ids_b[k] == number, grad_logit, 0.0)
    dense = dense.astype(jnp.bfloat16)

    def finish_b(n, inner):
        cols = columns(n)
        branch = mix(1, n, zsend_b, home_b, masks_b, share_b)
        term = dot(dense, router[:, cols])
        grad = (route_scale * branch + term) * gain[:, cols].astype(jnp.float32)
        grad_n[:, cols] = grad
        values = act_b[:, cols].astype(jnp.float32)
        return inner + jnp.sum(values * grad, axis=-1, keepdims=True)

    inner = lax.fori_loop(0, CHUNKS, finish_b, jnp.zeros((tokens, 1), jnp.float32))
    scale = inverse_b * inverse_b * inverse_b * (inner / width)

    def write_b(n, carry):
        cols = columns(n)
        values = act_b[:, cols].astype(jnp.float32)
        out = cot_b[:, cols].astype(jnp.float32) + inverse_b * grad_n[:, cols] - values * scale
        sect_b[:, cols] = out.astype(jnp.bfloat16)
        return carry

    lax.fori_loop(0, CHUNKS, write_b, 0)
    pb_copy = remote(sect_b, next_b, p_send.at[1], p_recv.at[1], last_pipe)
    pb_copy.start()

    for copy in w_copies:
        copy.wait_send()
    for i, into in enumerate((rows_a, rows_b, rows_c)):
        for step in range(experts):
            y_copy(i, into, step).wait_send()

    def drain(n, carry):
        down_copy(n).wait_send()
        yb_copy(0, n, ysend_a, yback_a).wait_send()
        yb_copy(1, n, ysend_b, yback_b).wait_send()
        for step in range(1, experts):
            zb_copy(0, n, zsend_a, home_a, step).wait_send()
            zb_copy(1, n, zsend_b, home_b, step).wait_send()
        return carry

    lax.fori_loop(0, CHUNKS, drain, 0)
    yc_copy.wait_send()
    for step in range(1, experts):
        zc_copy(step).wait_send()
    pa_copy.wait()
    pb_copy.wait()


def hand_out(from_a, from_b, into_a, into_b):
    into_a[...] = from_a[...]
    into_b[...] = from_b[...]


def per_device(act_a, ids_a, act_b, cot_b, ids_b, norm_gain, router, w_gate, w_up, w_down):
    n_expert = lax.axis_size("expert")
    n_pipe = lax.axis_size("pipe")
    experts = n_expert // SPLIT
    tokens, width = act_a.shape[1:]
    top = ids_a.shape[2]
    hidden = w_gate.shape[3]
    capacity = min(tokens, max(2, 5 * tokens * top // (4 * experts)))
    slot = -(-capacity // SLOT_ROWS) * SLOT_ROWS
    slots = experts * slot
    rows = 2 * slots
    sizes = (n_expert, n_pipe, experts, slot, top, width, hidden, tokens)

    def half(*dims):
        return pltpu.VMEM(dims, jnp.bfloat16)

    def full(*dims):
        return pltpu.VMEM(dims, jnp.float32)

    sem = pltpu.SemaphoreType.DMA
    block = (experts, slot, width)
    narrow = (experts, slot, LANES)
    pieces = (CHUNKS, experts, slot, width // CHUNKS)
    vmem = pl.BlockSpec(memory_space=pltpu.VMEM)
    anywhere = pl.BlockSpec(memory_space=pl.ANY)
    out = jax.ShapeDtypeStruct((tokens, width), jnp.bfloat16)
    next_a, next_b = pl.pallas_call(
        functools.partial(kernel, sizes),
        out_shape=(out, out),
        in_specs=[anywhere] * 3 + [vmem] * 4 + [anywhere] * 3,
        out_specs=(anywhere, anywhere),
        scratch_shapes=[
            half(width, hidden),
            half(width, hidden),
            half(hidden, width),
            half(width, hidden),
            half(width, hidden),
            half(hidden, width),
            half(tokens, width),
            half(tokens, width),
            half(tokens, width),
            half(tokens, width),
            half(*block),
            half(*block),
            half(*block),
            half(2, *block),
            half(2, *block),
            half(2, *block),
            full(rows, 2 * hidden),
            full(rows, 2 * hidden),
            full(rows, 2 * hidden),
            half(rows, 2 * hidden),
            half(rows, 2 * hidden),
            half(rows, 2 * hidden),
            half(rows, 2 * hidden),
            full(slots, width),
            full(slots, width),
            half(*pieces),
            half(*pieces),
            half(*narrow),
            half(*pieces),
            half(*pieces),
            half(*narrow),
            half(*pieces),
            half(*pieces),
            half(*narrow),
            half(*pieces),
            half(*pieces),
            half(*narrow),
            full(tokens, width),
            half(tokens, width),
            half(tokens, width),
            sem((6,)),
            sem((2 + CHUNKS,)),
            sem((2 + CHUNKS,)),
            sem((3, experts)),
            sem((3, experts)),
            sem((3, experts)),
            sem((3, experts)),
            sem((2, CHUNKS + 1)),
            sem((2, CHUNKS + 1)),
            sem((2, CHUNKS + 1, experts)),
            sem((2, CHUNKS + 1, experts)),
            sem((2,)),
            sem((2,)),
        ],
        compiler_params=pltpu.CompilerParams(
            collective_id=0, has_side_effects=True, vmem_limit_bytes=60 * 1024 * 1024
        ),
        cost_estimate=pl.CostEstimate(
            flops=2 * 9 * rows * width * hidden * 2,
            bytes_accessed=6 * width * hidden * 2,
            transcendentals=0,
        ),
    )(
        act_a[0],
        act_b[0],
        cot_b[0],
        ids_a[0].T,
        ids_b[0].T,
        norm_gain,
        router[0].T,
        w_gate[0, 0],
        w_up[0, 0],
        w_down[0, 0],
    )
    next_a, next_b = pl.pallas_call(
        hand_out,
        out_shape=(out, out),
        in_specs=[vmem] * 2,
        out_specs=(vmem, vmem),
    )(next_a, next_b)
    return (next_a[None], next_b[None])


SLOT_ROWS = 8


def solution(mesh):
    return jax.shard_map(
        per_device,
        mesh=mesh,
        in_specs=(
            P("pipe", "expert", None),
            P("pipe", "expert", None),
            P("pipe", "expert", None),
            P("pipe", "expert", None),
            P("pipe", "expert", None),
            P("pipe", None),
            P("pipe", None, None),
            P("pipe", "expert", None, None),
            P("pipe", "expert", None, None),
            P("pipe", "expert", None, None),
        ),
        out_specs=(P("pipe", "expert", None), P("pipe", "expert", None)),
        check_vma=False,
    )
```
